32 devices in a mesh: groups: 2 (over x), rows: 16 (over z, y, core).
Axes of the slice: x: 2, y: 2, z: 4, core: 2. Of those that a mesh axis runs over, the one named last changes fastest.
Arguments:
- frames: bfloat16 [2048, 3, 256], P(('groups', 'rows')), parts along dimension 0, may hold values from -6 to 6
- conv_tiles: bfloat16 [16, 27, 512, 128], P('rows'), may hold values from -0.0390625 to 0.0390625
- up_tiles: bfloat16 [16, 9, 256, 128], P('rows'), may hold values from -0.0625 to 0.0625
Outputs:
- upsampled_tiles: bfloat16 [32, 256, 128], P(('groups', 'rows')), parts along dimension 0
The draws below stay inside these ranges and needn't reach their ends.
There are 2 independent parts, one for each index of `groups`. The reference program is written for one: setup_inputs(seed, part) draws one part's arguments, and reference() takes and returns one part's arrays. A program takes and returns all parts, laid end to end along the dimension named above; an argument that names none is the same for every part. Nothing has to cross between parts.
All inputs are finite; a program needn't handle non-finite values.
Results may differ from the reference program's by a relative error of at most 0.009.
Values may be sent and summed in bfloat16 or wider, within the bound.
No kernel may reach another device: no remote copies, remote signals or barrier semaphores. Data moves between devices by JAX's collectives and lax.ppermute only.
A program may use at most 64 MiB of HBM per device.

```python
import jax
import jax.numpy as jnp

C = 1024
CO = 512
W = 64
SBLOCKS = 2
H = 4
V = 256
KI = 512
KO = 128
OB = 256
VB2 = 128
N_ROWS = 16


def level_of(key, extent, shards, least, top_value):
    def one(dim, shards_of):
        draws = jax.random.uniform(jax.random.fold_in(jax.random.fold_in(key, 6), dim), (shards_of,), jnp.float32, least / len(shards), top_value / len(shards))
        return jnp.repeat(jnp.exp(draws), extent[dim] // shards_of).reshape((-1,) + (1,) * (len(extent) - dim - 1))

    loudness = one(*shards[0])
    for cut in shards[1:]:
        loudness = loudness * one(*cut)
    return loudness


def bell_draw(own_key, dims, spread, limit, shards=(), held_as=jnp.bfloat16):
    entries = spread * jax.random.normal(own_key, dims, jnp.float32)
    if shards:
        entries = entries * level_of(own_key, dims, shards, -0.22, 0.18)
    return jnp.clip(entries, -limit, limit).astype(held_as)


def setup_inputs(seed: int = 0, part: int = 0) -> dict:
    streams_of = jax.random.split(jax.random.key(seed), 4)
    own_keys = jax.random.split(jax.random.fold_in(streams_of[3], part), 4)
    return {
        "frames": bell_draw(own_keys[0], (C, 3, V), 1.0, 6.0, ((0, 16),)),
        "conv_tiles": bell_draw(streams_of[1], (N_ROWS, 27, KI, KO), (27 * C) ** -0.5, 0.0390625, ((0, 16),)),
        "up_tiles": bell_draw(streams_of[2], (N_ROWS, 9, OB, KO), (9 * C) ** -0.5, 0.0625, ((0, 16),)),
    }


def shift_plane(planes, row_step, col_step):
    height = planes.shape[-2]
    width = planes.shape[-1]
    padded = jnp.pad(planes, [(0, 0)] * (planes.ndim - 2) + [(1, 1), (1, 1)])
    return padded[..., 1 + row_step:1 + row_step + height, 1 + col_step:1 + col_step + width]


def phase_groups(phase):
    if phase == 0:
        return [(-1, (0,)), (0, (1, 2))]
    return [(0, (0, 1)), (1, (2,))]


def reference(frames, conv_tiles, up_tiles):
    conv_weight = conv_tiles.reshape(SBLOCKS, 8, 27, KI, KO).transpose(2, 0, 3, 1, 4).reshape(27, C, C)
    volume = frames.reshape(C, 3, H, W)
    totals = jnp.zeros((C, V), jnp.float32)
    for kernel_tap in range(27):
        time_tap = kernel_tap // 9
        row_tap = (kernel_tap // 3) % 3
        col_tap = kernel_tap % 3
        plane = shift_plane(volume[:, time_tap], row_tap - 1, col_tap - 1).reshape(C, V)
        totals = totals + jnp.dot(conv_weight[kernel_tap].T, plane, preferred_element_type=jnp.float32)
    hidden = jax.nn.silu(totals).astype(jnp.bfloat16)
    hidden_planes = hidden.reshape(C, H, W)
    up_weight = up_tiles.reshape(SBLOCKS, 8, 9, OB, KO).transpose(2, 1, 4, 0, 3).reshape(9, C, CO)
    phase_rows = []
    for row_phase in range(2):
        phase_cols = []
        for col_phase in range(2):
            acc = jnp.zeros((CO, V), jnp.float32)
            for row_shift, row_taps in phase_groups(row_phase):
                for col_shift, col_taps in phase_groups(col_phase):
                    combined = jnp.zeros((C, CO), jnp.float32)
                    for row_tap in row_taps:
                        for col_tap in col_taps:
                            combined = combined + up_weight[3 * row_tap + col_tap].astype(jnp.float32)
                    combined = combined.astype(jnp.bfloat16)
                    plane = shift_plane(hidden_planes, row_shift, col_shift).reshape(C, V)
                    acc = acc + jnp.dot(combined.T, plane, preferred_element_type=jnp.float32)
            phase_cols.append(acc.reshape(CO, H, W))
        phase_rows.append(jnp.stack(phase_cols, 0))
    phased = jnp.stack(phase_rows, 0)
    result = phased.transpose(2, 3, 0, 4, 1).reshape(CO, 4 * V)
    rounded = result.astype(jnp.bfloat16)
    return rounded.reshape(SBLOCKS, OB, 8, VB2).transpose(0, 2, 1, 3).reshape(N_ROWS, OB, VB2)
```

```python
import functools

import jax
import jax.numpy as jnp
from jax import lax
from jax.experimental import pallas as pl
from jax.experimental.pallas import tpu as pltpu
from jax.sharding import PartitionSpec as P

W = 64
BF = jnp.bfloat16
F32 = jnp.float32
VMEM = pl.BlockSpec(memory_space=pltpu.VMEM)
SMEM = pl.BlockSpec(memory_space=pltpu.SMEM)
LIMIT = 32 * 2**20


def swap(block, mask):
    count = lax.axis_size("rows")
    return lax.ppermute(block, "rows", [(i, i ^ mask) for i in range(count)])


def local(body, outs, scratch, flops, moved, *args):
    return pl.pallas_call(
        body,
        out_shape=outs,
        in_specs=[SMEM] + [VMEM] * (len(args) - 1),
        out_specs=jax.tree.map(lambda _: VMEM, outs),
        scratch_shapes=scratch,
        compiler_params=pltpu.CompilerParams(vmem_limit_bytes=LIMIT),
        cost_estimate=pl.CostEstimate(flops=flops, bytes_accessed=moved, transcendentals=0),
    )(*args)


def phase_groups(phase):
    if phase == 0:
        return [(-1, (0,)), (0, (1, 2))]
    return [(0, (0, 1)), (1, (2,))]


def shift_cols(plane, step):
    if step == 0:
        return plane
    voxels = plane.shape[0]
    col = lax.broadcasted_iota(jnp.int32, plane.shape, 0) % W
    rolled = pltpu.roll(plane, (-step) % voxels, 0)
    return jnp.where((col + step >= 0) & (col + step < W), rolled, 0)


def shift_rows(plane, step):
    if step == 0:
        return plane
    zeros = jnp.zeros((W,) + plane.shape[1:], plane.dtype)
    if step > 0:
        return jnp.concatenate([plane[W:], zeros], 0)
    return jnp.concatenate([zeros, plane[:-W]], 0)


def phase_body(me_ref, tiles_ref, out_ref):
    taps = [tiles_ref[t].astype(F32).T for t in range(9)]
    depth = taps[0].shape[0]
    for p in range(2):
        for q in range(2):
            place = 0
            for _, row_taps in phase_groups(p):
                for _, col_taps in phase_groups(q):
                    total = None
                    for b in row_taps:
                        for e in col_taps:
                            tap = taps[3 * b + e]
                            total = tap if total is None else total + tap
                    out_ref[2 * p + q, place * depth : (place + 1) * depth, :] = total.astype(BF)
                    place += 1


def conv_body(share, me_ref, *refs):
    *piece_refs, weight_ref, full_ref, sent_ref, order_ref, columns_ref = refs
    frames_of, channels, voxels = order_ref.shape
    if len(piece_refs) == 1:
        order_ref[...] = piece_refs[0][...]
    else:
        part = channels // share
        for mask, piece_ref in enumerate(piece_refs):
            place = pl.multiple_of((me_ref[0] % share ^ mask) * part, part)
            order_ref[:, pl.ds(place, part), :] = piece_ref[...]
    for a in range(frames_of):
        columns_ref[:, a * channels : (a + 1) * channels] = order_ref[a].T
    products = {}
    taps = [(b, e) for e in range(3) for b in range(3)]
    for first in range(0, 9, 2):
        pair = taps[first : first + 2]
        weights = jnp.concatenate(
            [
                jnp.concatenate([weight_ref[9 * a + 3 * b + e] for a in range(frames_of)], 0)
                for b, e in pair
            ],
            1,
        )
        product = jnp.dot(columns_ref[...], weights, preferred_element_type=F32)
        for place, tap in enumerate(pair):
            filters = product.shape[1] // len(pair)
            products[tap] = product[:, place * filters : (place + 1) * filters]
    total = None
    for e in range(3):
        rows = sum(shift_rows(products[b, e], b - 1) for b in range(3))
        moved = shift_cols(rows, e - 1)
        total = moved if total is None else total + moved
    full_ref[...] = total
    sent_ref[...] = total.astype(BF)


def up_body(me_ref, *refs):
    *sum_refs, weight_ref, keep_ref, send_ref = refs
    pre = sum_refs[0][...]
    for other_ref in sum_refs[1:]:
        pre = pre + other_ref[...].astype(F32)
    hidden = pre / (1 + jnp.exp(-pre))
    hidden = hidden.astype(BF).astype(F32)
    planes = {}
    for v in (-1, 0, 1):
        shifted = shift_cols(hidden, v).astype(BF)
        for u in (-1, 0, 1):
            planes[u, v] = shift_rows(shifted, u)
    results = {}
    for p in range(2):
        for q in range(2):
            columns = jnp.concatenate(
                [planes[u, v] for u, _ in phase_groups(p) for v, _ in phase_groups(q)], 1
            )
            results[p, q] = jnp.dot(columns, weight_ref[2 * p + q], preferred_element_type=F32)
    halves, lines = keep_ref.shape[:2]
    upper = me_ref[0] % 2 == 1

    def line(f, k):
        row, p = divmod(f * lines + k, 2)
        return [results[p, q][row * W : (row + 1) * W] for q in range(2)]

    for half in range(halves):
        for k in range(lines):
            even, odd = line(2 * half, k), line(2 * half + 1, k)
            for q in range(2):
                cells = slice(q * W, (q + 1) * W)
                keep_ref[half, k, cells, :] = jnp.where(upper, odd[q], even[q])
                send_ref[half, k, cells, :] = jnp.where(upper, even[q], odd[q]).astype(BF)


def chip_body(me_ref, keep_ref, mate_ref, *out_refs):
    halves = keep_ref.shape[0]
    mine = me_ref[0] // 2 % halves
    for mask, out_ref in enumerate(out_refs):
        place = mine ^ mask
        total = keep_ref[place] + mate_ref[place].astype(F32)
        out_ref[...] = total.astype(out_ref.dtype)


def final_body(me_ref, own_ref, *refs):
    *other_refs, out_ref = refs
    total = own_ref[...]
    for other_ref in other_refs:
        total = total + other_ref[...].astype(F32)
    total = total.astype(BF)
    cell = lax.broadcasted_iota(jnp.int32, (2 * W, 2 * W), 0)
    place = lax.broadcasted_iota(jnp.int32, (2 * W, 2 * W), 1)
    spread = (place == 2 * (cell % W) + cell // W).astype(BF)
    for k in range(total.shape[0]):
        woven = lax.dot_general(
            total[k], spread, (((0,), (0,)), ((), ())), preferred_element_type=F32
        )
        out_ref[0, :, k * 2 * W : (k + 1) * 2 * W] = woven.astype(BF)


def on_device(frames, conv_tiles, up_tiles):
    index = lax.axis_index("rows")
    me = index.reshape(1).astype(jnp.int32)
    count = lax.axis_size("rows")
    part, frames_of, voxels = frames.shape
    taps, channels, filters = conv_tiles.shape[1:]
    outputs = up_tiles.shape[2]
    share = channels // part
    blocks = count // share
    lines = 2 * (voxels // W) // share
    shape = jax.ShapeDtypeStruct

    mine = frames.transpose(1, 0, 2)
    pieces = [mine] + [None] * (share - 1)
    for mask in range(2, share, 2):
        pieces[mask] = swap(mine, mask)
    for mask in range(0, share, 2):
        pieces[mask + 1] = swap(pieces[mask], 1)
    if part % 16:
        for mask in [1 << level for level in range(share.bit_length() - 1)]:
            pieces = [
                jnp.where(index & mask != 0, pieces[j ^ mask], pieces[j]) for j in range(share)
            ]
        pieces = [jnp.concatenate(pieces, 1)]

    phases = local(
        phase_body,
        shape((4, 4 * filters, outputs), BF),
        [],
        32 * filters * outputs,
        50 * filters * outputs,
        me,
        up_tiles[0],
    )
    partial, sent = local(
        functools.partial(conv_body, share),
        (shape((voxels, filters), F32), shape((voxels, filters), BF)),
        [
            pltpu.VMEM((frames_of, channels, voxels), BF),
            pltpu.VMEM((voxels, frames_of * channels), BF),
        ],
        2 * taps * channels * filters * voxels,
        2 * taps * channels * filters,
        me,
        *pieces,
        conv_tiles[0],
    )
    others = [swap(sent, share * block) for block in range(1, blocks)]
    keep, send = local(
        up_body,
        (
            shape((share // 2, lines, 2 * W, outputs), F32),
            shape((share // 2, lines, 2 * W, outputs), BF),
        ),
        [],
        32 * filters * outputs * voxels,
        32 * filters * outputs,
        me,
        partial,
        *others,
        phases,
    )
    mate = swap(send, 1)
    one = (lines, 2 * W, outputs)
    own, *leaving = local(
        chip_body,
        (shape(one, F32),) + (shape(one, BF),) * (share // 2 - 1),
        [],
        keep.size,
        6 * keep.size,
        me,
        keep,
        mate,
    )
    arrived = [swap(block, 2 * (mask + 1)) for mask, block in enumerate(leaving)]
    return local(
        final_body,
        shape((1, outputs, lines * 2 * W), BF),
        [],
        own.size,
        12 * own.size,
        me,
        own,
        *arrived,
    )


def solution(mesh):
    return jax.shard_map(
        on_device,
        mesh=mesh,
        in_specs=(
            P(("groups", "rows"), None, None),
            P("rows", None, None, None),
            P("rows", None, None, None),
        ),
        out_specs=P(("groups", "rows"), None, None),
        check_vma=False,
    )
```

```python
import functools

import jax
import jax.numpy as jnp
from jax import lax
from jax.experimental import pallas as pl
from jax.experimental.pallas import tpu as pltpu
from jax.sharding import PartitionSpec as P

W = 64
BF = jnp.bfloat16
F32 = jnp.float32
VMEM = pl.BlockSpec(memory_space=pltpu.VMEM)
SMEM = pl.BlockSpec(memory_space=pltpu.SMEM)
LIMIT = 32 * 2**20


def swap(block, mask):
    count = lax.axis_size("rows")
    return lax.ppermute(block, "rows", [(i, i ^ mask) for i in range(count)])


def local(body, outs, scratch, flops, moved, me, *args, ):
    return pl.pallas_call(
        body,
        out_shape=outs,
        in_specs=[SMEM] + [VMEM] * len(args),
        out_specs=jax.tree.map(lambda _: VMEM, outs),
        scratch_shapes=scratch,
        compiler_params=pltpu.CompilerParams(vmem_limit_bytes=LIMIT),
        cost_estimate=pl.CostEstimate(flops=flops, bytes_accessed=moved, transcendentals=0),
    )(me, *args)


def phase_groups(phase):
    if phase == 0:
        return [(-1, (0,)), (0, (1, 2))]
    return [(0, (0, 1)), (1, (2,))]


def shift_cols(plane, step):
    if step == 0:
        return plane
    voxels = plane.shape[0]
    col = lax.broadcasted_iota(jnp.int32, plane.shape, 0) % W
    rolled = pltpu.roll(plane, (-step) % voxels, 0)
    return jnp.where((col + step >= 0) & (col + step < W), rolled, 0)


def shift_rows(plane, step):
    if step == 0:
        return plane
    zeros = jnp.zeros((W,) + plane.shape[1:], plane.dtype)
    if step > 0:
        return jnp.concatenate([plane[W:], zeros], 0)
    return jnp.concatenate([zeros, plane[:-W]], 0)


def phase_body(me_ref, *refs):
    pairs = len(refs) // 2
    upper = me_ref[0] % 2 == 1
    for tiles_ref, out_ref in zip(refs[:pairs], refs[pairs:], strict=True):
        taps = [tiles_ref[t].astype(F32).T for t in range(9)]
        depth = taps[0].shape[0]
        for q in range(2):
            place = 0
            for u in range(2):
                for _, col_taps in phase_groups(q):
                    rows = slice(place * depth, (place + 1) * depth)
                    place += 1
                    totals = []
                    for p in range(2):
                        total = None
                        for b in phase_groups(p)[u][1]:
                            for e in col_taps:
                                tap = taps[3 * b + e]
                                total = tap if total is None else total + tap
                        totals.append(total)
                    if out_ref.shape[0] == 1:
                        totals = [jnp.where(upper, totals[1], totals[0])]
                    for p, total in enumerate(totals):
                        out_ref[p, q, rows, :] = total.astype(BF)


def conv_body(share, masks, first, last, me_ref, *refs):
    refs = list(refs)
    before_ref = None if first else refs.pop(0)
    weight_ref = refs.pop(0)
    pieces = [refs.pop(0) for _ in masks or (0,)]
    *out_refs, order_ref, columns_ref = refs
    frames_of, channels, voxels = order_ref.shape
    if masks:
        part = weight_ref.shape[1] // share
        me = me_ref[0] % share
        spans = []
        for i, mask in enumerate(masks):
            order_ref[:, i * part : (i + 1) * part, :] = pieces[i][...]
            spans.append(pl.ds(pl.multiple_of((me ^ mask) * part, part), part))
    else:
        order_ref[...] = pieces[0][...]
        spans = [slice(None)]
    for a in range(frames_of):
        columns_ref[:, a * channels : (a + 1) * channels] = order_ref[a].T
    products = [None] * 9
    for low in range(0, 9, 2):
        pair = range(low, min(low + 2, 9))
        weights = jnp.concatenate(
            [
                jnp.concatenate(
                    [weight_ref[9 * a + t, span, :] for a in range(frames_of) for span in spans], 0
                )
                for t in pair
            ],
            1,
        )
        product = jnp.dot(columns_ref[...], weights, preferred_element_type=F32)
        filters = product.shape[1] // len(pair)
        for i, t in enumerate(pair):
            own = product[:, i * filters : (i + 1) * filters]
            products[t] = own if first else before_ref[t] + own
    if not last:
        for t in range(9):
            out_refs[0][t] = products[t]
        return
    total = None
    for e in range(3):
        rows = sum(shift_rows(products[3 * b + e], b - 1) for b in range(3))
        moved = shift_cols(rows, e - 1)
        total = moved if total is None else total + moved
    out_refs[0][...] = total
    out_refs[1][...] = total.astype(BF)


def silu_body(me_ref, *refs):
    *sum_refs, hidden_ref = refs
    pre = sum_refs[0][...]
    for other_ref in sum_refs[1:]:
        pre = pre + other_ref[...].astype(F32)
    hidden_ref[...] = (pre / (1 + jnp.exp(-pre))).astype(BF)


def up_products(me_ref, hidden_ref, weight_ref, padded_ref, halves, lines):
    hidden = hidden_ref[...].astype(F32)
    voxels = hidden.shape[0]
    for i, v in enumerate((-1, 0, 1)):
        edge = jnp.zeros((W, hidden.shape[1]), BF)
        padded_ref[i, :W, :] = edge
        padded_ref[i, W + voxels :, :] = edge
        padded_ref[i, W : W + voxels, :] = shift_cols(hidden, v).astype(BF)
    upper = me_ref[0] % 2
    if lines == 1:
        blocks = [(0, halves, upper, [(half, 0) for half in range(halves)])]
    else:
        blocks = [
            (
                p,
                lines // 2,
                half * lines + upper * (lines // 2) + p,
                [(half, 2 * i + p) for i in range(lines // 2)],
            )
            for half in range(halves)
            for p in range(2)
        ]
    for p, count, base, places in blocks:
        for q in range(2):
            columns = []
            for u in range(2):
                start = pl.multiple_of((base + u) * W, W)
                for v, _ in phase_groups(q):
                    columns.append(padded_ref[v + 1, pl.ds(start, count * W), :])
            product = jnp.dot(
                jnp.concatenate(columns, 1), weight_ref[p, q], preferred_element_type=F32
            )
            for i, (half, k) in enumerate(places):
                yield half, k, slice(q * W, (q + 1) * W), product[i * W : (i + 1) * W]


def up_first_body(me_ref, hidden_ref, weight_ref, out_ref, padded_ref):
    halves, lines = out_ref.shape[:2]
    for half, k, cells, value in up_products(
        me_ref, hidden_ref, weight_ref, padded_ref, halves, lines
    ):
        out_ref[half, k, cells, :] = value


def up_second_body(me_ref, before_ref, hidden_ref, weight_ref, *refs):
    *out_refs, total_ref, padded_ref = refs
    halves, lines = before_ref.shape[:2]
    for half, k, cells, value in up_products(
        me_ref, hidden_ref, weight_ref, padded_ref, halves, lines
    ):
        total_ref[half, k, cells, :] = before_ref[half, k, cells, :] + value
    chip = me_ref[0] // 2 % halves
    for mask, out_ref in enumerate(out_refs):
        out_ref[...] = total_ref[chip ^ mask].astype(out_ref.dtype)


def final_body(me_ref, own_ref, *refs):
    *other_refs, out_ref = refs
    total = own_ref[...]
    for other_ref in other_refs:
        total = total + other_ref[...].astype(F32)
    total = total.astype(BF)
    cell = lax.broadcasted_iota(jnp.int32, (2 * W, 2 * W), 0)
    place = lax.broadcasted_iota(jnp.int32, (2 * W, 2 * W), 1)
    spread = (place == 2 * (cell % W) + cell // W).astype(BF)
    for k in range(total.shape[0]):
        woven = lax.dot_general(
            total[k], spread, (((0,), (0,)), ((), ())), preferred_element_type=F32
        )
        out_ref[0, :, k * 2 * W : (k + 1) * 2 * W] = woven.astype(BF)


def on_device(frames, conv_tiles, up_tiles):
    index = lax.axis_index("rows")
    me = index.reshape(1).astype(jnp.int32)
    count = lax.axis_size("rows")
    part, frames_of, voxels = frames.shape
    taps, channels, filters = conv_tiles.shape[1:]
    outputs = up_tiles.shape[2]
    share = channels // part
    blocks = count // share
    halves = share // 2
    lines = 2 * (voxels // W) // share
    shape = jax.ShapeDtypeStruct

    mine = frames.transpose(1, 0, 2)
    pieces = [mine, swap(mine, 1)] + [None] * (share - 2)
    for mask in range(2, share, 2):
        pieces[mask] = swap(mine, mask)
    tiles = up_tiles[0]
    weights = conv_tiles[0]
    if part % 16:
        for mask in range(2, share, 2):
            pieces[mask + 1] = swap(pieces[mask], 1)
        for mask in [1 << level for level in range(share.bit_length() - 1)]:
            pieces = [
                jnp.where(index & mask != 0, pieces[j ^ mask], pieces[j]) for j in range(share)
            ]
        steps = [()]
        pieces = [jnp.concatenate(pieces, 1)]
    else:
        far = share - 2
        near = list(range(2, far, 2))
        steps = [(0,), (1, far, far + 1, *near), tuple(mask + 1 for mask in near)]

    before = []
    for i, masks in enumerate(steps):
        first, last = i == 0, i == len(steps) - 1
        parts = [pieces[mask] for mask in masks] or pieces
        depth = sum(block.shape[1] for block in parts)
        outs = [shape((voxels, filters), F32), shape((voxels, filters), BF)]
        if not last:
            outs = [shape((9, voxels, filters), F32)]
        scratch = [
            pltpu.VMEM((frames_of, depth, voxels), BF),
            pltpu.VMEM((voxels, frames_of * depth), BF),
        ]
        done = local(
            functools.partial(conv_body, share, masks, first, last),
            tuple(outs),
            scratch,
            2 * taps * depth * filters * voxels,
            2 * taps * depth * filters,
            me,
            *before,
            weights,
            *parts,
        )
        before = done[:1]
        if first and not last:
            pieces[far], *before = lax.optimization_barrier((pieces[far], *before))
            for mask in range(2, share, 2):
                pieces[mask + 1] = swap(pieces[mask], 1)
    partial, sent = done
    partial, tiles = lax.optimization_barrier((partial, tiles))
    mate_tiles = swap(tiles, 1)
    others = [swap(sent, share * block) for block in range(1, blocks)]
    some = (min(lines, 2), 2, 4 * filters, outputs)
    keep, mate_phases = local(
        phase_body,
        (shape(some, BF), shape(some, BF)),
        [],
        64 * filters * outputs,
        68 * filters * outputs,
        me,
        up_tiles[0],
        mate_tiles,
    )
    hidden = local(
        silu_body,
        shape((voxels, filters), BF),
        [],
        8 * voxels * filters,
        8 * voxels * filters,
        me,
        partial,
        *others,
    )
    mate_hidden = swap(hidden, 1)
    one = (lines, 2 * W, outputs)
    padded = pltpu.VMEM((3, voxels + 2 * W, filters), BF)
    work = 16 * filters * outputs * voxels
    first = local(
        up_first_body,
        shape((halves, *one), F32),
        [padded],
        work,
        16 * filters * outputs,
        me,
        hidden,
        keep,
    )
    own, *leaving = local(
        up_second_body,
        (shape(one, F32),) + (shape(one, BF),) * (halves - 1),
        [pltpu.VMEM((halves, *one), F32), padded],
        work,
        16 * filters * outputs,
        me,
        first,
        mate_hidden,
        mate_phases,
    )
    arrived = [swap(block, 2 * (mask + 1)) for mask, block in enumerate(leaving)]
    return local(
        final_body,
        shape((1, outputs, lines * 2 * W), BF),
        [],
        own.size,
        12 * own.size,
        me,
        own,
        *arrived,
    )


def solution(mesh):
    return jax.shard_map(
        on_device,
        mesh=mesh,
        in_specs=(
            P(("groups", "rows"), None, None),
            P("rows", None, None, None),
            P("rows", None, None, None),
        ),
        out_specs=P(("groups", "rows"), None, None),
        check_vma=False,
    )
```

```python
import functools

import jax
import jax.numpy as jnp
from jax import lax
from jax.experimental import pallas as pl
from jax.experimental.pallas import tpu as pltpu
from jax.sharding import PartitionSpec as P

W = 64
BF = jnp.bfloat16
F32 = jnp.float32
VMEM = pl.BlockSpec(memory_space=pltpu.VMEM)
SMEM = pl.BlockSpec(memory_space=pltpu.SMEM)
HBM = pl.BlockSpec(memory_space=pltpu.HBM)
LIMIT = 32 * 2**20


def swap(block, mask):
    count = lax.axis_size("rows")
    return lax.ppermute(block, "rows", [(i, i ^ mask) for i in range(count)])


def local(body, outs, scratch, flops, moved, me, *args, in_hbm=()):
    return pl.pallas_call(
        body,
        out_shape=outs,
        in_specs=[SMEM] + [HBM if i in in_hbm else VMEM for i in range(len(args))],
        out_specs=jax.tree.map(lambda _: VMEM, outs),
        scratch_shapes=scratch,
        compiler_params=pltpu.CompilerParams(vmem_limit_bytes=LIMIT),
        cost_estimate=pl.CostEstimate(flops=flops, bytes_accessed=moved, transcendentals=0),
    )(me, *args)


def phase_groups(phase):
    if phase == 0:
        return [(-1, (0,)), (0, (1, 2))]
    return [(0, (0, 1)), (1, (2,))]


def shift_cols(plane, step):
    if step == 0:
        return plane
    voxels = plane.shape[0]
    col = lax.broadcasted_iota(jnp.int32, plane.shape, 0) % W
    rolled = pltpu.roll(plane, (-step) % voxels, 0)
    return jnp.where((col + step >= 0) & (col + step < W), rolled, 0)


def shift_rows(plane, step):
    if step == 0:
        return plane
    zeros = jnp.zeros((W,) + plane.shape[1:], plane.dtype)
    if step > 0:
        return jnp.concatenate([plane[W:], zeros], 0)
    return jnp.concatenate([zeros, plane[:-W]], 0)


def phase_body(me_ref, tiles_ref, out_ref):
    upper = me_ref[0] % 2 == 1
    taps = [tiles_ref[t].astype(F32).T for t in range(9)]
    depth = taps[0].shape[0]
    for q in range(2):
        place = 0
        for u in range(2):
            for _, col_taps in phase_groups(q):
                rows = slice(place * depth, (place + 1) * depth)
                place += 1
                totals = []
                for p in range(2):
                    total = None
                    for b in phase_groups(p)[u][1]:
                        for e in col_taps:
                            tap = taps[3 * b + e]
                            total = tap if total is None else total + tap
                    totals.append(total)
                if out_ref.shape[0] == 1:
                    totals = [jnp.where(upper, totals[1], totals[0])]
                for p, total in enumerate(totals):
                    out_ref[p, q, rows, :] = total.astype(BF)


def conv_body(share, masks, first, last, me_ref, *refs):
    refs = list(refs)
    before_ref = None if first else refs.pop(0)
    weight_ref = refs.pop(0)
    pieces = [refs.pop(0) for _ in masks or (0,)]
    *out_refs, order_ref, columns_ref = refs
    frames_of, channels, voxels = order_ref.shape
    if masks:
        part = weight_ref.shape[1] // share
        me = me_ref[0] % share
        spans = []
        for i, mask in enumerate(masks):
            order_ref[:, i * part : (i + 1) * part, :] = pieces[i][...]
            spans.append(pl.ds(pl.multiple_of((me ^ mask) * part, part), part))
    else:
        order_ref[...] = pieces[0][...]
        spans = [slice(None)]
    for a in range(frames_of):
        columns_ref[:, a * channels : (a + 1) * channels] = order_ref[a].T
    products = [None] * 9
    for low in range(0, 9, 2):
        pair = range(low, min(low + 2, 9))
        weights = jnp.concatenate(
            [
                jnp.concatenate(
                    [weight_ref[9 * a + t, span, :] for a in range(frames_of) for span in spans], 0
                )
                for t in pair
            ],
            1,
        )
        product = jnp.dot(columns_ref[...], weights, preferred_element_type=F32)
        filters = product.shape[1] // len(pair)
        for i, t in enumerate(pair):
            own = product[:, i * filters : (i + 1) * filters]
            products[t] = own if first else before_ref[t] + own
    if not last:
        for t in range(9):
            out_refs[0][t] = products[t]
        return
    total = None
    for e in range(3):
        rows = sum(shift_rows(products[3 * b + e], b - 1) for b in range(3))
        moved = shift_cols(rows, e - 1)
        total = moved if total is None else total + moved
    out_refs[0][...] = total
    out_refs[1][...] = total.astype(BF)


def silu_body(me_ref, *refs):
    *sum_refs, hidden_ref = refs
    pre = sum_refs[0][...]
    for other_ref in sum_refs[1:]:
        pre = pre + other_ref[...].astype(F32)
    hidden_ref[...] = (pre / (1 + jnp.exp(-pre))).astype(BF)


def up_products(me_ref, hidden_ref, weight_ref, padded_ref, halves, lines):
    hidden = hidden_ref[...].astype(F32)
    voxels = hidden.shape[0]
    for i, v in enumerate((-1, 0, 1)):
        edge = jnp.zeros((W, hidden.shape[1]), BF)
        padded_ref[i, :W, :] = edge
        padded_ref[i, W + voxels :, :] = edge
        padded_ref[i, W : W + voxels, :] = shift_cols(hidden, v).astype(BF)
    upper = me_ref[0] % 2
    if lines == 1:
        blocks = [(0, halves, upper, [(half, 0) for half in range(halves)])]
    else:
        blocks = [
            (
                p,
                lines // 2,
                half * lines + upper * (lines // 2) + p,
                [(half, 2 * i + p) for i in range(lines // 2)],
            )
            for half in range(halves)
            for p in range(2)
        ]
    for p, count, base, places in blocks:
        for q in range(2):
            columns = []
            for u in range(2):
                start = pl.multiple_of((base + u) * W, W)
                for v, _ in phase_groups(q):
                    columns.append(padded_ref[v + 1, pl.ds(start, count * W), :])
            product = jnp.dot(
                jnp.concatenate(columns, 1), weight_ref[p, q], preferred_element_type=F32
            )
            for i, (half, k) in enumerate(places):
                yield half, k, slice(q * W, (q + 1) * W), product[i * W : (i + 1) * W]


def up_first_body(me_ref, hidden_ref, weight_ref, out_ref, padded_ref):
    halves, lines = out_ref.shape[:2]
    for half, k, cells, value in up_products(
        me_ref, hidden_ref, weight_ref, padded_ref, halves, lines
    ):
        out_ref[half, k, cells, :] = value


def up_second_body(me_ref, before_ref, hidden_ref, weight_ref, *refs):
    *out_refs, total_ref, padded_ref = refs
    halves, lines = before_ref.shape[:2]
    for half, k, cells, value in up_products(
        me_ref, hidden_ref, weight_ref, padded_ref, halves, lines
    ):
        total_ref[half, k, cells, :] = before_ref[half, k, cells, :] + value
    chip = me_ref[0] // 2 % halves
    for mask, out_ref in enumerate(out_refs):
        out_ref[...] = total_ref[chip ^ mask].astype(out_ref.dtype)


def spread_body(me_ref, out_ref):
    cell = lax.broadcasted_iota(jnp.int32, out_ref.shape, 0)
    place = lax.broadcasted_iota(jnp.int32, out_ref.shape, 1)
    out_ref[...] = (place == 2 * (cell % W) + cell // W).astype(BF)


def final_body(me_ref, spread_ref, own_ref, *refs):
    *other_refs, out_ref = refs
    total = own_ref[...]
    for other_ref in other_refs:
        total = total + other_ref[...].astype(F32)
    total = total.astype(BF)
    for k in range(total.shape[0]):
        woven = lax.dot_general(
            total[k], spread_ref[...], (((0,), (0,)), ((), ())), preferred_element_type=F32
        )
        out_ref[0, :, k * 2 * W : (k + 1) * 2 * W] = woven.astype(BF)


def on_device(frames, conv_tiles, up_tiles):
    index = lax.axis_index("rows")
    me = index.reshape(1).astype(jnp.int32)
    count = lax.axis_size("rows")
    part, frames_of, voxels = frames.shape
    taps, channels, filters = conv_tiles.shape[1:]
    outputs = up_tiles.shape[2]
    share = channels // part
    blocks = count // share
    halves = share // 2
    lines = 2 * (voxels // W) // share
    shape = jax.ShapeDtypeStruct

    mine = frames.transpose(1, 0, 2)
    pieces = [mine] + [None] * (share - 1)
    far = share - 2
    near = list(range(2, far, 2))
    for mask in range(2, share, 2):
        pieces[mask] = swap(mine, mask)
    spread = local(spread_body, shape((2 * W, 2 * W), BF), [], 2**33, 2**25, me)
    mate_tiles = swap(up_tiles[0], 1)
    pieces[far], spread, mate_tiles = lax.optimization_barrier(
        (pieces[far], spread, mate_tiles)
    )
    pieces[0], spread = lax.optimization_barrier((mine, spread))
    for mask in range(0, share, 2):
        pieces[mask + 1] = swap(pieces[mask], 1)
    weights = conv_tiles[0]
    if part % 16:
        for mask in [1 << level for level in range(share.bit_length() - 1)]:
            pieces = [
                jnp.where(index & mask != 0, pieces[j ^ mask], pieces[j]) for j in range(share)
            ]
        steps = [()]
        pieces = [jnp.concatenate(pieces, 1)]
    else:
        steps = [(0, 1, far, far + 1, *near), tuple(mask + 1 for mask in near)]

    before = []
    for i, masks in enumerate(steps):
        first, last = i == 0, i == len(steps) - 1
        parts = [pieces[mask] for mask in masks] or pieces
        depth = sum(block.shape[1] for block in parts)
        outs = [shape((voxels, filters), F32), shape((voxels, filters), BF)]
        if not last:
            outs = [shape((9, voxels, filters), F32)]
        scratch = [
            pltpu.VMEM((frames_of, depth, voxels), BF),
            pltpu.VMEM((voxels, frames_of * depth), BF),
        ]
        done = local(
            functools.partial(conv_body, share, masks, first, last),
            tuple(outs),
            scratch,
            2 * taps * depth * filters * voxels,
            2 * taps * depth * filters,
            me,
            *before,
            weights,
            *parts,
        )
        before = done[:1]
    partial, sent = done
    others = [swap(sent, share * block) for block in range(1, blocks)]
    phases = functools.partial(
        local,
        phase_body,
        shape((min(lines, 2), 2, 4 * filters, outputs), BF),
        [],
        32 * filters * outputs,
        34 * filters * outputs,
        me,
    )
    partial, tiles, mate_tiles = lax.optimization_barrier((partial, up_tiles[0], mate_tiles))
    keep, mate_phases = phases(tiles), phases(mate_tiles)
    others[0], keep, mate_phases = lax.optimization_barrier((others[0], keep, mate_phases))
    hidden = local(
        silu_body,
        shape((voxels, filters), BF),
        [],
        8 * voxels * filters,
        8 * voxels * filters,
        me,
        partial,
        *others,
    )
    mate_hidden = swap(hidden, 1)
    one = (lines, 2 * W, outputs)
    padded = pltpu.VMEM((3, voxels + 2 * W, filters), BF)
    work = 16 * filters * outputs * voxels
    first = local(
        up_first_body,
        shape((halves, *one), F32),
        [padded],
        work,
        16 * filters * outputs,
        me,
        hidden,
        keep,
    )
    own, *leaving = local(
        up_second_body,
        (shape(one, F32),) + (shape(one, BF),) * (halves - 1),
        [pltpu.VMEM((halves, *one), F32), padded],
        work,
        16 * filters * outputs,
        me,
        first,
        mate_hidden,
        mate_phases,
    )
    arrived = [swap(block, 2 * (mask + 1)) for mask, block in enumerate(leaving)]
    return local(
        final_body,
        shape((1, outputs, lines * 2 * W), BF),
        [],
        own.size,
        12 * own.size,
        me,
        spread,
        own,
        *arrived,
    )


def solution(mesh):
    return jax.shard_map(
        on_device,
        mesh=mesh,
        in_specs=(
            P(("groups", "rows"), None, None),
            P("rows", None, None, None),
            P("rows", None, None, None),
        ),
        out_specs=P(("groups", "rows"), None, None),
        check_vma=False,
    )
```

```python
import functools

import jax
import jax.numpy as jnp
from jax import lax
from jax.experimental import pallas as pl
from jax.experimental.pallas import tpu as pltpu
from jax.sharding import PartitionSpec as P

W = 64
BF = jnp.bfloat16
F32 = jnp.float32
VMEM = pl.BlockSpec(memory_space=pltpu.VMEM)
SMEM = pl.BlockSpec(memory_space=pltpu.SMEM)
LIMIT = 32 * 2**20


def swap(block, mask):
    count = lax.axis_size("rows")
    return lax.ppermute(block, "rows", [(i, i ^ mask) for i in range(count)])


def local(body, outs, scratch, flops, moved, me, *args):
    return pl.pallas_call(
        body,
        out_shape=outs,
        in_specs=[SMEM] + [VMEM] * len(args),
        out_specs=jax.tree.map(lambda _: VMEM, outs),
        scratch_shapes=scratch,
        compiler_params=pltpu.CompilerParams(vmem_limit_bytes=LIMIT),
        cost_estimate=pl.CostEstimate(flops=flops, bytes_accessed=moved, transcendentals=0),
    )(me, *args)


def farthest_first(chips):
    return (chips - 1, *range(1, chips - 1))


def phase_groups(phase):
    if phase == 0:
        return [(-1, (0,)), (0, (1, 2))]
    return [(0, (0, 1)), (1, (2,))]


def shift_cols(plane, step):
    if step == 0:
        return plane
    voxels = plane.shape[0]
    col = lax.broadcasted_iota(jnp.int32, plane.shape, 0) % W
    rolled = pltpu.roll(plane, (-step) % voxels, 0)
    return jnp.where((col + step >= 0) & (col + step < W), rolled, 0)


def shift_rows(plane, step):
    if step == 0:
        return plane
    zeros = jnp.zeros((W,) + plane.shape[1:], plane.dtype)
    if step > 0:
        return jnp.concatenate([plane[W:], zeros], 0)
    return jnp.concatenate([zeros, plane[:-W]], 0)


def phase_body(me_ref, tiles_ref, out_ref):
    upper = me_ref[0] % 2 == 1
    taps = [tiles_ref[t].astype(F32).T for t in range(9)]
    depth = taps[0].shape[0]
    for q in range(2):
        place = 0
        for u in range(2):
            for _, col_taps in phase_groups(q):
                rows = slice(place * depth, (place + 1) * depth)
                place += 1
                totals = []
                for p in range(2):
                    total = None
                    for b in phase_groups(p)[u][1]:
                        for e in col_taps:
                            tap = taps[3 * b + e]
                            total = tap if total is None else total + tap
                    totals.append(total)
                if out_ref.shape[0] == 1:
                    totals = [jnp.where(upper, totals[1], totals[0])]
                for p, total in enumerate(totals):
                    out_ref[p, q, rows, :] = total.astype(BF)


def conv_body(share, masks, first, last, me_ref, *refs):
    refs = list(refs)
    before_ref = None if first else refs.pop(0)
    weight_ref = refs.pop(0)
    pieces = [refs.pop(0) for _ in masks or (0,)]
    *out_refs, order_ref, columns_ref = refs
    frames_of, channels, voxels = order_ref.shape
    if masks:
        part = weight_ref.shape[1] // share
        me = me_ref[0] % share
        spans = []
        for i, mask in enumerate(masks):
            order_ref[:, i * part : (i + 1) * part, :] = pieces[i][...]
            spans.append(pl.ds(pl.multiple_of((me ^ mask) * part, part), part))
    else:
        order_ref[...] = pieces[0][...]
        spans = [slice(None)]
    for a in range(frames_of):
        columns_ref[:, a * channels : (a + 1) * channels] = order_ref[a].T
    products = [None] * 9
    for low in range(0, 9, 2):
        pair = range(low, min(low + 2, 9))
        weights = jnp.concatenate(
            [
                jnp.concatenate(
                    [weight_ref[9 * a + t, span, :] for a in range(frames_of) for span in spans], 0
                )
                for t in pair
            ],
            1,
        )
        product = jnp.dot(columns_ref[...], weights, preferred_element_type=F32)
        filters = product.shape[1] // len(pair)
        for i, t in enumerate(pair):
            own = product[:, i * filters : (i + 1) * filters]
            products[t] = own if first else before_ref[t] + own
    if not last:
        for t in range(9):
            out_refs[0][t] = products[t]
        return
    total = None
    for e in range(3):
        rows = sum(shift_rows(products[3 * b + e], b - 1) for b in range(3))
        moved = shift_cols(rows, e - 1)
        total = moved if total is None else total + moved
    out_refs[0][...] = total
    out_refs[1][...] = total.astype(BF)


def silu_body(me_ref, *refs):
    *sum_refs, hidden_ref = refs
    pre = sum_refs[0][...]
    for other_ref in sum_refs[1:]:
        pre = pre + other_ref[...].astype(F32)
    hidden_ref[...] = (pre / (1 + jnp.exp(-pre))).astype(BF)


def up_products(me_ref, hidden_ref, weight_ref, padded_ref, halves, lines):
    hidden = hidden_ref[...].astype(F32)
    voxels = hidden.shape[0]
    for i, v in enumerate((-1, 0, 1)):
        edge = jnp.zeros((W, hidden.shape[1]), BF)
        padded_ref[i, :W, :] = edge
        padded_ref[i, W + voxels :, :] = edge
        padded_ref[i, W : W + voxels, :] = shift_cols(hidden, v).astype(BF)
    upper = me_ref[0] % 2
    if lines == 1:
        blocks = [(0, halves, upper, [(half, 0) for half in range(halves)])]
    else:
        blocks = [
            (
                p,
                lines // 2,
                half * lines + upper * (lines // 2) + p,
                [(half, 2 * i + p) for i in range(lines // 2)],
            )
            for half in range(halves)
            for p in range(2)
        ]
    for p, count, base, places in blocks:
        for q in range(2):
            columns = []
            for u in range(2):
                start = pl.multiple_of((base + u) * W, W)
                for v, _ in phase_groups(q):
                    columns.append(padded_ref[v + 1, pl.ds(start, count * W), :])
            product = jnp.dot(
                jnp.concatenate(columns, 1), weight_ref[p, q], preferred_element_type=F32
            )
            for i, (half, k) in enumerate(places):
                yield half, k, slice(q * W, (q + 1) * W), product[i * W : (i + 1) * W]


def up_first_body(me_ref, hidden_ref, weight_ref, out_ref, padded_ref):
    halves, lines = out_ref.shape[:2]
    for half, k, cells, value in up_products(
        me_ref, hidden_ref, weight_ref, padded_ref, halves, lines
    ):
        out_ref[half, k, cells, :] = value


def up_second_body(me_ref, before_ref, hidden_ref, weight_ref, *refs):
    *out_refs, total_ref, padded_ref = refs
    halves, lines = before_ref.shape[:2]
    for half, k, cells, value in up_products(
        me_ref, hidden_ref, weight_ref, padded_ref, halves, lines
    ):
        total_ref[half, k, cells, :] = before_ref[half, k, cells, :] + value
    chip = me_ref[0] // 2 % halves
    own_ref, *leaving_refs = out_refs
    own_ref[...] = total_ref[chip]
    for mask, out_ref in zip(farthest_first(halves), leaving_refs, strict=True):
        out_ref[...] = total_ref[chip ^ mask].astype(BF)


def spread_body(me_ref, out_ref):
    cell = lax.broadcasted_iota(jnp.int32, out_ref.shape, 0)
    place = lax.broadcasted_iota(jnp.int32, out_ref.shape, 1)
    out_ref[...] = (place == 2 * (cell % W) + cell // W).astype(BF)


def final_body(me_ref, spread_ref, own_ref, *refs):
    *other_refs, out_ref = refs
    total = own_ref[...]
    for other_ref in other_refs:
        total = total + other_ref[...].astype(F32)
    total = total.astype(BF)
    for k in range(total.shape[0]):
        woven = lax.dot_general(
            total[k], spread_ref[...], (((0,), (0,)), ((), ())), preferred_element_type=F32
        )
        out_ref[0, :, k * 2 * W : (k + 1) * 2 * W] = woven.astype(BF)


def on_device(frames, conv_tiles, up_tiles):
    index = lax.axis_index("rows")
    me = index.reshape(1).astype(jnp.int32)
    count = lax.axis_size("rows")
    part, frames_of, voxels = frames.shape
    taps, channels, filters = conv_tiles.shape[1:]
    outputs = up_tiles.shape[2]
    share = channels // part
    blocks = count // share
    halves = share // 2
    lines = 2 * (voxels // W) // share
    shape = jax.ShapeDtypeStruct

    mine = frames.transpose(1, 0, 2)
    pieces = [mine] + [None] * (share - 1)
    far = share - 2
    near = list(range(2, far, 2))
    for mask in range(2, share, 2):
        pieces[mask] = swap(mine, mask)
    spread = local(spread_body, shape((2 * W, 2 * W), BF), [], 2**33, 2**25, me)
    mate_tiles = swap(up_tiles[0], 1)
    pieces[far], spread, mate_tiles = lax.optimization_barrier(
        (pieces[far], spread, mate_tiles)
    )
    pieces[0], spread = lax.optimization_barrier((mine, spread))
    for mask in range(0, share, 2):
        pieces[mask + 1] = swap(pieces[mask], 1)
    weights = conv_tiles[0]
    if part % 16:
        for mask in [1 << level for level in range(share.bit_length() - 1)]:
            pieces = [
                jnp.where(index & mask != 0, pieces[j ^ mask], pieces[j]) for j in range(share)
            ]
        steps = [()]
        pieces = [jnp.concatenate(pieces, 1)]
    else:
        steps = [(0, 1, far, far + 1, *near), tuple(mask + 1 for mask in near)]

    before = []
    for i, masks in enumerate(steps):
        first, last = i == 0, i == len(steps) - 1
        parts = [pieces[mask] for mask in masks] or pieces
        depth = sum(block.shape[1] for block in parts)
        outs = [shape((voxels, filters), F32), shape((voxels, filters), BF)]
        if not last:
            outs = [shape((9, voxels, filters), F32)]
        scratch = [
            pltpu.VMEM((frames_of, depth, voxels), BF),
            pltpu.VMEM((voxels, frames_of * depth), BF),
        ]
        done = local(
            functools.partial(conv_body, share, masks, first, last),
            tuple(outs),
            scratch,
            2 * taps * depth * filters * voxels,
            2 * taps * depth * filters,
            me,
            *before,
            weights,
            *parts,
        )
        before = done[:1]
    partial, sent = done
    others = [swap(sent, share * block) for block in range(1, blocks)]
    phases = functools.partial(
        local,
        phase_body,
        shape((min(lines, 2), 2, 4 * filters, outputs), BF),
        [],
        32 * filters * outputs,
        34 * filters * outputs,
        me,
    )
    partial, tiles, mate_tiles = lax.optimization_barrier((partial, up_tiles[0], mate_tiles))
    keep, mate_phases = phases(tiles), phases(mate_tiles)
    others[0], keep, mate_phases = lax.optimization_barrier((others[0], keep, mate_phases))
    hidden = local(
        silu_body,
        shape((voxels, filters), BF),
        [],
        8 * voxels * filters,
        8 * voxels * filters,
        me,
        partial,
        *others,
    )
    mate_hidden = swap(hidden, 1)
    one = (lines, 2 * W, outputs)
    padded = pltpu.VMEM((3, voxels + 2 * W, filters), BF)
    work = 16 * filters * outputs * voxels
    first = local(
        up_first_body,
        shape((halves, *one), F32),
        [padded],
        work,
        16 * filters * outputs,
        me,
        hidden,
        keep,
    )
    own, *leaving = local(
        up_second_body,
        (shape(one, F32),) + (shape(one, BF),) * (halves - 1),
        [pltpu.VMEM((halves, *one), F32), padded],
        work,
        16 * filters * outputs,
        me,
        first,
        mate_hidden,
        mate_phases,
    )
    arrived = [
        swap(block, 2 * mask) for mask, block in zip(farthest_first(halves), leaving, strict=True)
    ]
    return local(
        final_body,
        shape((1, outputs, lines * 2 * W), BF),
        [],
        own.size,
        12 * own.size,
        me,
        spread,
        own,
        *arrived,
    )


def solution(mesh):
    return jax.shard_map(
        on_device,
        mesh=mesh,
        in_specs=(
            P(("groups", "rows"), None, None),
            P("rows", None, None, None),
            P("rows", None, None, None),
        ),
        out_specs=P(("groups", "rows"), None, None),
        check_vma=False,
    )
```

```python
import functools

import jax
import jax.numpy as jnp
from jax import lax
from jax.experimental import pallas as pl
from jax.experimental.pallas import tpu as pltpu
from jax.sharding import PartitionSpec as P

W = 64
BF = jnp.bfloat16
F32 = jnp.float32
VMEM = pl.BlockSpec(memory_space=pltpu.VMEM)
SMEM = pl.BlockSpec(memory_space=pltpu.SMEM)
LIMIT = 32 * 2**20


def swap(block, mask):
    count = lax.axis_size("rows")
    return lax.ppermute(block, "rows", [(i, i ^ mask) for i in range(count)])


def local(body, outs, scratch, flops, moved, me, *args):
    return pl.pallas_call(
        body,
        out_shape=outs,
        in_specs=[SMEM] + [VMEM] * len(args),
        out_specs=jax.tree.map(lambda _: VMEM, outs),
        scratch_shapes=scratch,
        compiler_params=pltpu.CompilerParams(vmem_limit_bytes=LIMIT),
        cost_estimate=pl.CostEstimate(flops=flops, bytes_accessed=moved, transcendentals=0),
    )(me, *args)


def farthest_first(chips):
    return (chips - 1, *range(1, chips - 1))


def phase_groups(phase):
    if phase == 0:
        return [(-1, (0,)), (0, (1, 2))]
    return [(0, (0, 1)), (1, (2,))]


def shift_cols(plane, step):
    if step == 0:
        return plane
    voxels = plane.shape[0]
    col = lax.broadcasted_iota(jnp.int32, plane.shape, 0) % W
    rolled = pltpu.roll(plane, (-step) % voxels, 0)
    return jnp.where((col + step >= 0) & (col + step < W), rolled, 0)


def shift_rows(plane, step):
    if step == 0:
        return plane
    zeros = jnp.zeros((W,) + plane.shape[1:], plane.dtype)
    if step > 0:
        return jnp.concatenate([plane[W:], zeros], 0)
    return jnp.concatenate([zeros, plane[:-W]], 0)


def phase_body(me_ref, tiles_ref, out_ref):
    upper = me_ref[0] % 2 == 1
    taps = [tiles_ref[t].astype(F32).T for t in range(9)]
    depth = taps[0].shape[0]
    for q in range(2):
        place = 0
        for u in range(2):
            for _, col_taps in phase_groups(q):
                rows = slice(place * depth, (place + 1) * depth)
                place += 1
                totals = []
                for p in range(2):
                    total = None
                    for b in phase_groups(p)[u][1]:
                        for e in col_taps:
                            tap = taps[3 * b + e]
                            total = tap if total is None else total + tap
                    totals.append(total)
                if out_ref.shape[0] == 1:
                    totals = [jnp.where(upper, totals[1], totals[0])]
                for p, total in enumerate(totals):
                    out_ref[p, q, rows, :] = total.astype(BF)


def conv_body(share, masks, first, last, me_ref, *refs):
    refs = list(refs)
    before_ref = None if first else refs.pop(0)
    weight_ref = refs.pop(0)
    pieces = [refs.pop(0) for _ in masks or (0,)]
    *out_refs, order_ref = refs
    frames_of, _, voxels = pieces[0].shape
    channels = order_ref.shape[0] // frames_of
    if masks:
        part = weight_ref.shape[1] // share
        me = me_ref[0] % share
        spans = [pl.ds(pl.multiple_of((me ^ mask) * part, part), part) for mask in masks]
    else:
        spans = [slice(None)]
    for a in range(frames_of):
        for i, piece_ref in enumerate(pieces):
            place = a * channels + i * piece_ref.shape[1]
            order_ref[place : place + piece_ref.shape[1], :] = piece_ref[a]
    columns = order_ref[...].T
    products = [None] * 9
    for low in range(0, 9, 2):
        pair = range(low, min(low + 2, 9))
        weights = jnp.concatenate(
            [
                jnp.concatenate(
                    [weight_ref[9 * a + t, span, :] for a in range(frames_of) for span in spans], 0
                )
                for t in pair
            ],
            1,
        )
        product = jnp.dot(columns, weights, preferred_element_type=F32)
        filters = product.shape[1] // len(pair)
        for i, t in enumerate(pair):
            own = product[:, i * filters : (i + 1) * filters]
            products[t] = own if first else before_ref[t] + own
    if not last:
        for t in range(9):
            out_refs[0][t] = products[t]
        return
    total = None
    for e in range(3):
        rows = sum(shift_rows(products[3 * b + e], b - 1) for b in range(3))
        moved = shift_cols(rows, e - 1)
        total = moved if total is None else total + moved
    out_refs[0][...] = total
    out_refs[1][...] = total.astype(BF)


def silu_body(me_ref, *refs):
    *sum_refs, hidden_ref = refs
    pre = sum_refs[0][...]
    for other_ref in sum_refs[1:]:
        pre = pre + other_ref[...].astype(F32)
    hidden_ref[...] = (pre / (1 + jnp.exp(-pre))).astype(BF)


def up_products(me_ref, hidden_ref, weight_ref, padded_ref, halves, lines):
    hidden = hidden_ref[...].astype(F32)
    voxels = hidden.shape[0]
    for i, v in enumerate((-1, 0, 1)):
        edge = jnp.zeros((W, hidden.shape[1]), BF)
        padded_ref[i, :W, :] = edge
        padded_ref[i, W + voxels :, :] = edge
        padded_ref[i, W : W + voxels, :] = shift_cols(hidden, v).astype(BF)
    upper = me_ref[0] % 2
    if lines == 1:
        blocks = [(0, halves, upper, [(half, 0) for half in range(halves)])]
    else:
        blocks = [
            (
                p,
                lines // 2,
                half * lines + upper * (lines // 2) + p,
                [(half, 2 * i + p) for i in range(lines // 2)],
            )
            for half in range(halves)
            for p in range(2)
        ]
    for p, count, base, places in blocks:
        for q in range(2):
            columns = []
            for u in range(2):
                start = pl.multiple_of((base + u) * W, W)
                for v, _ in phase_groups(q):
                    columns.append(padded_ref[v + 1, pl.ds(start, count * W), :])
            product = jnp.dot(
                jnp.concatenate(columns, 1), weight_ref[p, q], preferred_element_type=F32
            )
            for i, (half, k) in enumerate(places):
                yield half, k, slice(q * W, (q + 1) * W), product[i * W : (i + 1) * W]


def up_first_body(me_ref, hidden_ref, weight_ref, out_ref, padded_ref):
    halves, lines = out_ref.shape[:2]
    for half, k, cells, value in up_products(
        me_ref, hidden_ref, weight_ref, padded_ref, halves, lines
    ):
        out_ref[half, k, cells, :] = value


def up_second_body(me_ref, before_ref, hidden_ref, weight_ref, *refs):
    *out_refs, total_ref, padded_ref = refs
    halves, lines = before_ref.shape[:2]
    for half, k, cells, value in up_products(
        me_ref, hidden_ref, weight_ref, padded_ref, halves, lines
    ):
        total_ref[half, k, cells, :] = before_ref[half, k, cells, :] + value
    chip = me_ref[0] // 2 % halves
    own_ref, *leaving_refs = out_refs
    own_ref[...] = total_ref[chip]
    for mask, out_ref in zip(farthest_first(halves), leaving_refs, strict=True):
        out_ref[...] = total_ref[chip ^ mask].astype(BF)


def spread_body(me_ref, out_ref):
    cell = lax.broadcasted_iota(jnp.int32, out_ref.shape, 0)
    place = lax.broadcasted_iota(jnp.int32, out_ref.shape, 1)
    out_ref[...] = (place == 2 * (cell % W) + cell // W).astype(BF)


def final_body(me_ref, spread_ref, own_ref, *refs):
    *other_refs, out_ref, line_ref = refs
    total = own_ref[...]
    for other_ref in other_refs:
        total = total + other_ref[...].astype(F32)
    total = total.astype(BF)
    outputs = total.shape[2]
    for k in range(total.shape[0]):
        places = slice(k * 2 * W, (k + 1) * 2 * W)
        whole = outputs // 128
        for i in range(whole):
            block = total[k, :, i * 128 : (i + 1) * 128].astype(F32)
            for q in range(2):
                line_ref[k, i, pl.ds(q, W, stride=2), :] = block[q * W : (q + 1) * W]
        for i in range(whole):
            out_ref[0, i * 128 : (i + 1) * 128, places] = line_ref[k, i].T.astype(BF)
        if outputs % 128:
            woven = lax.dot_general(
                total[k, :, whole * 128 :],
                spread_ref[...],
                (((0,), (0,)), ((), ())),
                preferred_element_type=F32,
            )
            out_ref[0, whole * 128 :, places] = woven.astype(BF)


def on_device(frames, conv_tiles, up_tiles):
    index = lax.axis_index("rows")
    me = index.reshape(1).astype(jnp.int32)
    count = lax.axis_size("rows")
    part, frames_of, voxels = frames.shape
    taps, channels, filters = conv_tiles.shape[1:]
    outputs = up_tiles.shape[2]
    share = channels // part
    blocks = count // share
    halves = share // 2
    lines = 2 * (voxels // W) // share
    shape = jax.ShapeDtypeStruct

    mine = frames.transpose(1, 0, 2)
    pieces = [mine] + [None] * (share - 1)
    far = share - 2
    near = list(range(2, far, 2))
    for mask in range(2, share, 2):
        pieces[mask] = swap(mine, mask)
    spread = local(spread_body, shape((2 * W, 2 * W), BF), [], 2**33, 2**25, me)
    mate_tiles = swap(up_tiles[0], 1)
    pieces[far], spread, mate_tiles = lax.optimization_barrier(
        (pieces[far], spread, mate_tiles)
    )
    pieces[0], spread = lax.optimization_barrier((mine, spread))
    for mask in range(0, share, 2):
        pieces[mask + 1] = swap(pieces[mask], 1)
    weights = conv_tiles[0]
    if part % 16:
        for mask in [1 << level for level in range(share.bit_length() - 1)]:
            pieces = [
                jnp.where(index & mask != 0, pieces[j ^ mask], pieces[j]) for j in range(share)
            ]
        steps = [()]
        pieces = [jnp.concatenate(pieces, 1)]
    else:
        steps = [(0, 1, far, far + 1, *near), tuple(mask + 1 for mask in near)]

    before = []
    for i, masks in enumerate(steps):
        first, last = i == 0, i == len(steps) - 1
        parts = [pieces[mask] for mask in masks] or pieces
        depth = sum(block.shape[1] for block in parts)
        outs = [shape((voxels, filters), F32), shape((voxels, filters), BF)]
        if not last:
            outs = [shape((9, voxels, filters), F32)]
        done = local(
            functools.partial(conv_body, share, masks, first, last),
            tuple(outs),
            [pltpu.VMEM((frames_of * depth, voxels), BF)],
            2 * taps * depth * filters * voxels,
            2 * taps * depth * filters,
            me,
            *before,
            weights,
            *parts,
        )
        before = done[:1]
    partial, sent = done
    others = [swap(sent, share * block) for block in range(1, blocks)]
    phases = functools.partial(
        local,
        phase_body,
        shape((min(lines, 2), 2, 4 * filters, outputs), BF),
        [],
        32 * filters * outputs,
        34 * filters * outputs,
        me,
    )
    partial, tiles, mate_tiles = lax.optimization_barrier((partial, up_tiles[0], mate_tiles))
    keep, mate_phases = phases(tiles), phases(mate_tiles)
    others[0], keep, mate_phases = lax.optimization_barrier((others[0], keep, mate_phases))
    hidden = local(
        silu_body,
        shape((voxels, filters), BF),
        [],
        8 * voxels * filters,
        8 * voxels * filters,
        me,
        partial,
        *others,
    )
    mate_hidden = swap(hidden, 1)
    one = (lines, 2 * W, outputs)
    padded = pltpu.VMEM((3, voxels + 2 * W, filters), BF)
    work = 16 * filters * outputs * voxels
    first = local(
        up_first_body,
        shape((halves, *one), F32),
        [padded],
        work,
        16 * filters * outputs,
        me,
        hidden,
        keep,
    )
    own, *leaving = local(
        up_second_body,
        (shape(one, F32),) + (shape(one, BF),) * (halves - 1),
        [pltpu.VMEM((halves, *one), F32), padded],
        work,
        16 * filters * outputs,
        me,
        first,
        mate_hidden,
        mate_phases,
    )
    arrived = [
        swap(block, 2 * mask) for mask, block in zip(farthest_first(halves), leaving, strict=True)
    ]
    return local(
        final_body,
        shape((1, outputs, lines * 2 * W), BF),
        [pltpu.VMEM((lines, max(outputs // 128, 1), 2 * W, 128), F32)],
        own.size,
        12 * own.size,
        me,
        spread,
        own,
        *arrived,
    )


def solution(mesh):
    return jax.shard_map(
        on_device,
        mesh=mesh,
        in_specs=(
            P(("groups", "rows"), None, None),
            P("rows", None, None, None),
            P("rows", None, None, None),
        ),
        out_specs=P(("groups", "rows"), None, None),
        check_vma=False,
    )
```

```python
import functools

import jax
import jax.numpy as jnp
from jax import lax
from jax.experimental import pallas as pl
from jax.experimental.pallas import tpu as pltpu
from jax.sharding import PartitionSpec as P

W = 64
BF = jnp.bfloat16
F32 = jnp.float32
VMEM = pl.BlockSpec(memory_space=pltpu.VMEM)
SMEM = pl.BlockSpec(memory_space=pltpu.SMEM)
LIMIT = 32 * 2**20


def swap(block, mask):
    count = lax.axis_size("rows")
    return lax.ppermute(block, "rows", [(i, i ^ mask) for i in range(count)])


def local(body, outs, scratch, flops, moved, me, *args):
    return pl.pallas_call(
        body,
        out_shape=outs,
        in_specs=[SMEM] + [VMEM] * len(args),
        out_specs=jax.tree.map(lambda _: VMEM, outs),
        scratch_shapes=scratch,
        compiler_params=pltpu.CompilerParams(vmem_limit_bytes=LIMIT),
        cost_estimate=pl.CostEstimate(flops=flops, bytes_accessed=moved, transcendentals=0),
    )(me, *args)


def farthest_first(chips):
    return (chips - 1, *range(1, chips - 1))


def phase_groups(phase):
    if phase == 0:
        return [(-1, (0,)), (0, (1, 2))]
    return [(0, (0, 1)), (1, (2,))]


def shift_cols(plane, step):
    if step == 0:
        return plane
    voxels = plane.shape[0]
    col = lax.broadcasted_iota(jnp.int32, plane.shape, 0) % W
    rolled = pltpu.roll(plane, (-step) % voxels, 0)
    return jnp.where((col + step >= 0) & (col + step < W), rolled, 0)


def shift_rows(plane, step):
    if step == 0:
        return plane
    zeros = jnp.zeros((W,) + plane.shape[1:], plane.dtype)
    if step > 0:
        return jnp.concatenate([plane[W:], zeros], 0)
    return jnp.concatenate([zeros, plane[:-W]], 0)


def phase_body(me_ref, tiles_ref, out_ref):
    upper = me_ref[0] % 2 == 1
    taps = [tiles_ref[t].astype(F32).T for t in range(9)]
    depth = taps[0].shape[0]
    for q in range(2):
        place = 0
        for u in range(2):
            for _, col_taps in phase_groups(q):
                rows = slice(place * depth, (place + 1) * depth)
                place += 1
                totals = []
                for p in range(2):
                    total = None
                    for b in phase_groups(p)[u][1]:
                        for e in col_taps:
                            tap = taps[3 * b + e]
                            total = tap if total is None else total + tap
                    totals.append(total)
                if out_ref.shape[0] == 1:
                    totals = [jnp.where(upper, totals[1], totals[0])]
                for p, total in enumerate(totals):
                    out_ref[p, q, rows, :] = total.astype(BF)


def conv_body(share, masks, first, last, me_ref, *refs):
    refs = list(refs)
    before_ref = None if first else refs.pop(0)
    weight_ref = refs.pop(0)
    pieces = []
    while len(pieces) < max(len(masks), 1):
        ref = refs.pop(0)
        pieces += [ref] if len(ref.shape) == 3 else [ref.at[i] for i in range(ref.shape[0])]
    *out_refs, order_ref = refs
    frames_of, _, voxels = pieces[0].shape
    channels = order_ref.shape[0] // frames_of
    if masks:
        part = weight_ref.shape[1] // share
        me = me_ref[0] % share
        spans = [pl.ds(pl.multiple_of((me ^ mask) * part, part), part) for mask in masks]
    else:
        spans = [slice(None)]
    for a in range(frames_of):
        for i, piece_ref in enumerate(pieces):
            place = a * channels + i * piece_ref.shape[1]
            order_ref[place : place + piece_ref.shape[1], :] = piece_ref[a]
    columns = order_ref[...].T
    products = [None] * 9
    for low in range(0, 9, 2):
        pair = range(low, min(low + 2, 9))
        weights = jnp.concatenate(
            [
                jnp.concatenate(
                    [weight_ref[9 * a + t, span, :] for a in range(frames_of) for span in spans], 0
                )
                for t in pair
            ],
            1,
        )
        product = jnp.dot(columns, weights, preferred_element_type=F32)
        filters = product.shape[1] // len(pair)
        for i, t in enumerate(pair):
            own = product[:, i * filters : (i + 1) * filters]
            products[t] = own if first else before_ref[t] + own
    if not last:
        for t in range(9):
            out_refs[0][t] = products[t]
        return
    total = None
    for e in range(3):
        rows = sum(shift_rows(products[3 * b + e], b - 1) for b in range(3))
        moved = shift_cols(rows, e - 1)
        total = moved if total is None else total + moved
    out_refs[0][...] = total
    out_refs[1][...] = total.astype(BF)


def pack_body(me_ref, *refs):
    *block_refs, out_ref = refs
    for i, block_ref in enumerate(block_refs):
        out_ref[i] = block_ref[...]


def silu_body(me_ref, *refs):
    *sum_refs, hidden_ref = refs
    pre = sum_refs[0][...]
    for other_ref in sum_refs[1:]:
        pre = pre + other_ref[...].astype(F32)
    hidden_ref[...] = (pre / (1 + jnp.exp(-pre))).astype(BF)


def up_products(me_ref, hidden_ref, weight_ref, padded_ref, halves, lines):
    hidden = hidden_ref[...].astype(F32)
    voxels = hidden.shape[0]
    for i, v in enumerate((-1, 0, 1)):
        edge = jnp.zeros((W, hidden.shape[1]), BF)
        padded_ref[i, :W, :] = edge
        padded_ref[i, W + voxels :, :] = edge
        padded_ref[i, W : W + voxels, :] = shift_cols(hidden, v).astype(BF)
    upper = me_ref[0] % 2
    if lines == 1:
        blocks = [(0, halves, upper, [(half, 0) for half in range(halves)])]
    else:
        blocks = [
            (
                p,
                lines // 2,
                half * lines + upper * (lines // 2) + p,
                [(half, 2 * i + p) for i in range(lines // 2)],
            )
            for half in range(halves)
            for p in range(2)
        ]
    for p, count, base, places in blocks:
        for q in range(2):
            columns = []
            for u in range(2):
                start = pl.multiple_of((base + u) * W, W)
                for v, _ in phase_groups(q):
                    columns.append(padded_ref[v + 1, pl.ds(start, count * W), :])
            product = jnp.dot(
                jnp.concatenate(columns, 1), weight_ref[p, q], preferred_element_type=F32
            )
            for i, (half, k) in enumerate(places):
                yield half, k, slice(q * W, (q + 1) * W), product[i * W : (i + 1) * W]


def up_first_body(me_ref, hidden_ref, weight_ref, out_ref, padded_ref):
    halves, lines = out_ref.shape[:2]
    for half, k, cells, value in up_products(
        me_ref, hidden_ref, weight_ref, padded_ref, halves, lines
    ):
        out_ref[half, k, cells, :] = value


def up_second_body(me_ref, before_ref, hidden_ref, weight_ref, *refs):
    *out_refs, total_ref, padded_ref = refs
    halves, lines = before_ref.shape[:2]
    for half, k, cells, value in up_products(
        me_ref, hidden_ref, weight_ref, padded_ref, halves, lines
    ):
        total_ref[half, k, cells, :] = before_ref[half, k, cells, :] + value
    chip = me_ref[0] // 2 % halves
    own_ref, *leaving_refs = out_refs
    own_ref[...] = total_ref[chip]
    for mask, out_ref in zip(farthest_first(halves), leaving_refs, strict=True):
        out_ref[...] = total_ref[chip ^ mask].astype(BF)


def spread_body(me_ref, out_ref):
    cell = lax.broadcasted_iota(jnp.int32, out_ref.shape, 0)
    place = lax.broadcasted_iota(jnp.int32, out_ref.shape, 1)
    out_ref[...] = (place == 2 * (cell % W) + cell // W).astype(BF)


def final_body(me_ref, spread_ref, own_ref, *refs):
    *other_refs, out_ref, line_ref = refs
    total = own_ref[...]
    for other_ref in other_refs:
        total = total + other_ref[...].astype(F32)
    total = total.astype(BF)
    outputs = total.shape[2]
    for k in range(total.shape[0]):
        places = slice(k * 2 * W, (k + 1) * 2 * W)
        whole = outputs // 128
        for i in range(whole):
            block = total[k, :, i * 128 : (i + 1) * 128].astype(F32)
            for q in range(2):
                line_ref[k, i, pl.ds(q, W, stride=2), :] = block[q * W : (q + 1) * W]
        for i in range(whole):
            out_ref[0, i * 128 : (i + 1) * 128, places] = line_ref[k, i].T.astype(BF)
        if outputs % 128:
            woven = lax.dot_general(
                total[k, :, whole * 128 :],
                spread_ref[...],
                (((0,), (0,)), ((), ())),
                preferred_element_type=F32,
            )
            out_ref[0, whole * 128 :, places] = woven.astype(BF)


def on_device(frames, conv_tiles, up_tiles):
    index = lax.axis_index("rows")
    me = index.reshape(1).astype(jnp.int32)
    count = lax.axis_size("rows")
    part, frames_of, voxels = frames.shape
    taps, channels, filters = conv_tiles.shape[1:]
    outputs = up_tiles.shape[2]
    share = channels // part
    blocks = count // share
    halves = share // 2
    lines = 2 * (voxels // W) // share
    shape = jax.ShapeDtypeStruct

    mine = frames.transpose(1, 0, 2)
    pieces = [mine] + [None] * (share - 1)
    far = share - 2
    near = list(range(2, far, 2))
    for mask in range(2, share, 2):
        pieces[mask] = swap(mine, mask)
    spread = local(spread_body, shape((2 * W, 2 * W), BF), [], 2**33, 2**25, me)
    mate_tiles = swap(up_tiles[0], 1)
    pieces[far], spread, mate_tiles = lax.optimization_barrier(
        (pieces[far], spread, mate_tiles)
    )
    pieces[0], spread = lax.optimization_barrier((mine, spread))
    weights = conv_tiles[0]
    if part % 16:
        for mask in range(0, share, 2):
            pieces[mask + 1] = swap(pieces[mask], 1)
        for mask in [1 << level for level in range(share.bit_length() - 1)]:
            pieces = [
                jnp.where(index & mask != 0, pieces[j ^ mask], pieces[j]) for j in range(share)
            ]
        steps = [((), [jnp.concatenate(pieces, 1)])]
    else:

        def mates(masks):
            blocks = [pieces[mask] for mask in masks]
            packed = shape((len(blocks), *mine.shape), BF)
            return swap(local(pack_body, packed, [], 0, 2 * packed.size, me, *blocks), 1)

        near_mates, far_mates = mates(near), mates((0, far))
        direct = (0, far, *near)
        steps = [
            ((*direct, 1, far + 1), [pieces[mask] for mask in direct] + [far_mates]),
            (tuple(mask + 1 for mask in near), [near_mates]),
        ]

    before = []
    for i, (masks, parts) in enumerate(steps):
        first, last = i == 0, i == len(steps) - 1
        depth = part * len(masks) or channels
        outs = [shape((voxels, filters), F32), shape((voxels, filters), BF)]
        if not last:
            outs = [shape((9, voxels, filters), F32)]
        done = local(
            functools.partial(conv_body, share, masks, first, last),
            tuple(outs),
            [pltpu.VMEM((frames_of * depth, voxels), BF)],
            2 * taps * depth * filters * voxels,
            2 * taps * depth * filters,
            me,
            *before,
            weights,
            *parts,
        )
        before = done[:1]
    partial, sent = done
    others = [swap(sent, share * block) for block in range(1, blocks)]
    phases = functools.partial(
        local,
        phase_body,
        shape((min(lines, 2), 2, 4 * filters, outputs), BF),
        [],
        32 * filters * outputs,
        34 * filters * outputs,
        me,
    )
    partial, tiles, mate_tiles = lax.optimization_barrier((partial, up_tiles[0], mate_tiles))
    keep, mate_phases = phases(tiles), phases(mate_tiles)
    others[0], keep, mate_phases = lax.optimization_barrier((others[0], keep, mate_phases))
    hidden = local(
        silu_body,
        shape((voxels, filters), BF),
        [],
        8 * voxels * filters,
        8 * voxels * filters,
        me,
        partial,
        *others,
    )
    mate_hidden = swap(hidden, 1)
    one = (lines, 2 * W, outputs)
    padded = pltpu.VMEM((3, voxels + 2 * W, filters), BF)
    work = 16 * filters * outputs * voxels
    first = local(
        up_first_body,
        shape((halves, *one), F32),
        [padded],
        work,
        16 * filters * outputs,
        me,
        hidden,
        keep,
    )
    own, *leaving = local(
        up_second_body,
        (shape(one, F32),) + (shape(one, BF),) * (halves - 1),
        [pltpu.VMEM((halves, *one), F32), padded],
        work,
        16 * filters * outputs,
        me,
        first,
        mate_hidden,
        mate_phases,
    )
    arrived = [
        swap(block, 2 * mask) for mask, block in zip(farthest_first(halves), leaving, strict=True)
    ]
    return local(
        final_body,
        shape((1, outputs, lines * 2 * W), BF),
        [pltpu.VMEM((lines, max(outputs // 128, 1), 2 * W, 128), F32)],
        own.size,
        12 * own.size,
        me,
        spread,
        own,
        *arrived,
    )


def solution(mesh):
    return jax.shard_map(
        on_device,
        mesh=mesh,
        in_specs=(
            P(("groups", "rows"), None, None),
            P("rows", None, None, None),
            P("rows", None, None, None),
        ),
        out_specs=P(("groups", "rows"), None, None),
        check_vma=False,
    )
```

```python
import functools

import jax
import jax.numpy as jnp
from jax import lax
from jax.experimental import pallas as pl
from jax.experimental.pallas import tpu as pltpu
from jax.sharding import PartitionSpec as P

W = 64
BF = jnp.bfloat16
F32 = jnp.float32
VMEM = pl.BlockSpec(memory_space=pltpu.VMEM)
SMEM = pl.BlockSpec(memory_space=pltpu.SMEM)
LIMIT = 32 * 2**20


def swap(block, mask):
    count = lax.axis_size("rows")
    return lax.ppermute(block, "rows", [(i, i ^ mask) for i in range(count)])


def local(body, outs, scratch, flops, moved, me, *args):
    return pl.pallas_call(
        body,
        out_shape=outs,
        in_specs=[SMEM] + [VMEM] * len(args),
        out_specs=jax.tree.map(lambda _: VMEM, outs),
        scratch_shapes=scratch,
        compiler_params=pltpu.CompilerParams(vmem_limit_bytes=LIMIT),
        cost_estimate=pl.CostEstimate(flops=flops, bytes_accessed=moved, transcendentals=0),
    )(me, *args)


def farthest_first(chips):
    return (chips - 1, *range(1, chips - 1))


def phase_groups(phase):
    if phase == 0:
        return [(-1, (0,)), (0, (1, 2))]
    return [(0, (0, 1)), (1, (2,))]


def shift_cols(plane, step):
    if step == 0:
        return plane
    voxels = plane.shape[0]
    col = lax.broadcasted_iota(jnp.int32, plane.shape, 0) % W
    rolled = pltpu.roll(plane, (-step) % voxels, 0)
    return jnp.where((col + step >= 0) & (col + step < W), rolled, 0)


def shift_rows(plane, step):
    if step == 0:
        return plane
    zeros = jnp.zeros((W,) + plane.shape[1:], plane.dtype)
    if step > 0:
        return jnp.concatenate([plane[W:], zeros], 0)
    return jnp.concatenate([zeros, plane[:-W]], 0)


def phase_body(me_ref, tiles_ref, out_ref):
    upper = me_ref[0] % 2 == 1
    taps = [tiles_ref[t].astype(F32).T for t in range(9)]
    depth = taps[0].shape[0]
    for q in range(2):
        place = 0
        for u in range(2):
            for _, col_taps in phase_groups(q):
                rows = slice(place * depth, (place + 1) * depth)
                place += 1
                totals = []
                for p in range(2):
                    total = None
                    for b in phase_groups(p)[u][1]:
                        for e in col_taps:
                            tap = taps[3 * b + e]
                            total = tap if total is None else total + tap
                    totals.append(total)
                if out_ref.shape[0] == 1:
                    totals = [jnp.where(upper, totals[1], totals[0])]
                for p, total in enumerate(totals):
                    out_ref[p, q, rows, :] = total.astype(BF)


def conv_body(share, masks, first, last, me_ref, *refs):
    refs = list(refs)
    before_ref = None if first else refs.pop(0)
    weight_ref = refs.pop(0)
    pieces = [refs.pop(0) for _ in masks or (0,)]
    *out_refs, order_ref = refs
    frames_of, _, voxels = pieces[0].shape
    channels = order_ref.shape[0] // frames_of
    if masks:
        part = weight_ref.shape[1] // share
        me = me_ref[0] % share
        spans = [pl.ds(pl.multiple_of((me ^ mask) * part, part), part) for mask in masks]
    else:
        spans = [slice(None)]
    for a in range(frames_of):
        for i, piece_ref in enumerate(pieces):
            place = a * channels + i * piece_ref.shape[1]
            order_ref[place : place + piece_ref.shape[1], :] = piece_ref[a]
    columns = order_ref[...].T
    products = [None] * 9
    for low in range(0, 9, 2):
        pair = range(low, min(low + 2, 9))
        weights = jnp.concatenate(
            [
                jnp.concatenate(
                    [weight_ref[9 * a + t, span, :] for a in range(frames_of) for span in spans], 0
                )
                for t in pair
            ],
            1,
        )
        product = jnp.dot(columns, weights, preferred_element_type=F32)
        filters = product.shape[1] // len(pair)
        for i, t in enumerate(pair):
            own = product[:, i * filters : (i + 1) * filters]
            products[t] = own if first else before_ref[t] + own
    if not last:
        for t in range(9):
            out_refs[0][t] = products[t]
        return
    total = None
    for e in range(3):
        rows = sum(shift_rows(products[3 * b + e], b - 1) for b in range(3))
        moved = shift_cols(rows, e - 1)
        total = moved if total is None else total + moved
    out_refs[0][...] = total
    out_refs[1][...] = total.astype(BF)


def silu_body(me_ref, *refs):
    *sum_refs, hidden_ref = refs
    pre = sum_refs[0][...]
    for other_ref in sum_refs[1:]:
        pre = pre + other_ref[...].astype(F32)
    hidden_ref[...] = (pre / (1 + jnp.exp(-pre))).astype(BF)


def up_products(me_ref, hidden_ref, weight_ref, padded_ref, halves, lines):
    hidden = hidden_ref[...].astype(F32)
    voxels = hidden.shape[0]
    for i, v in enumerate((-1, 0, 1)):
        edge = jnp.zeros((W, hidden.shape[1]), BF)
        padded_ref[i, :W, :] = edge
        padded_ref[i, W + voxels :, :] = edge
        plane = shift_cols(hidden, v).astype(BF) if v else hidden_ref[...]
        padded_ref[i, W : W + voxels, :] = plane
    upper = me_ref[0] % 2
    if lines == 1:
        blocks = [(0, halves, upper, [(half, 0) for half in range(halves)])]
    else:
        blocks = [
            (
                p,
                lines // 2,
                half * lines + upper * (lines // 2) + p,
                [(half, 2 * i + p) for i in range(lines // 2)],
            )
            for half in range(halves)
            for p in range(2)
        ]
    for p, count, base, places in blocks:
        for q in range(2):
            columns = []
            for u in range(2):
                start = pl.multiple_of((base + u) * W, W)
                for v, _ in phase_groups(q):
                    columns.append(padded_ref[v + 1, pl.ds(start, count * W), :])
            product = jnp.dot(
                jnp.concatenate(columns, 1), weight_ref[p, q], preferred_element_type=F32
            )
            for i, (half, k) in enumerate(places):
                yield half, k, slice(q * W, (q + 1) * W), product[i * W : (i + 1) * W]


def up_first_body(me_ref, hidden_ref, weight_ref, out_ref, padded_ref):
    halves, lines = out_ref.shape[:2]
    for half, k, cells, value in up_products(
        me_ref, hidden_ref, weight_ref, padded_ref, halves, lines
    ):
        out_ref[half, k, cells, :] = value


def up_second_body(me_ref, before_ref, hidden_ref, weight_ref, *refs):
    *out_refs, total_ref, padded_ref = refs
    halves, lines = before_ref.shape[:2]
    for half, k, cells, value in up_products(
        me_ref, hidden_ref, weight_ref, padded_ref, halves, lines
    ):
        total_ref[half, k, cells, :] = before_ref[half, k, cells, :] + value
    chip = me_ref[0] // 2 % halves
    own_ref, *leaving_refs = out_refs
    own_ref[...] = total_ref[chip]
    for mask, out_ref in zip(farthest_first(halves), leaving_refs, strict=True):
        out_ref[...] = total_ref[chip ^ mask].astype(BF)


def spread_body(me_ref, out_ref):
    cell = lax.broadcasted_iota(jnp.int32, out_ref.shape, 0)
    place = lax.broadcasted_iota(jnp.int32, out_ref.shape, 1)
    out_ref[...] = (place == 2 * (cell % W) + cell // W).astype(BF)


def final_body(me_ref, spread_ref, own_ref, *refs):
    *other_refs, out_ref, line_ref = refs
    total = own_ref[...]
    for other_ref in other_refs:
        total = total + other_ref[...].astype(F32)
    total = total.astype(BF)
    outputs = total.shape[2]
    for k in range(total.shape[0]):
        places = slice(k * 2 * W, (k + 1) * 2 * W)
        whole = outputs // 128
        for i in range(whole):
            block = total[k, :, i * 128 : (i + 1) * 128].astype(F32)
            for q in range(2):
                line_ref[k, i, pl.ds(q, W, stride=2), :] = block[q * W : (q + 1) * W]
        for i in range(whole):
            out_ref[0, i * 128 : (i + 1) * 128, places] = line_ref[k, i].T.astype(BF)
        if outputs % 128:
            woven = lax.dot_general(
                total[k, :, whole * 128 :],
                spread_ref[...],
                (((0,), (0,)), ((), ())),
                preferred_element_type=F32,
            )
            out_ref[0, whole * 128 :, places] = woven.astype(BF)


def on_device(frames, conv_tiles, up_tiles):
    index = lax.axis_index("rows")
    me = index.reshape(1).astype(jnp.int32)
    count = lax.axis_size("rows")
    part, frames_of, voxels = frames.shape
    taps, channels, filters = conv_tiles.shape[1:]
    outputs = up_tiles.shape[2]
    share = channels // part
    blocks = count // share
    halves = share // 2
    lines = 2 * (voxels // W) // share
    shape = jax.ShapeDtypeStruct

    mine = frames.transpose(1, 0, 2)
    pieces = [mine] + [None] * (share - 1)
    far = share - 2
    near = list(range(2, far, 2))
    for mask in range(2, share, 2):
        pieces[mask] = swap(mine, mask)
    spread = local(spread_body, shape((2 * W, 2 * W), BF), [], 2**33, 2**25, me)
    mate_tiles = swap(up_tiles[0], 1)
    pieces[far], spread, mate_tiles = lax.optimization_barrier(
        (pieces[far], spread, mate_tiles)
    )
    pieces[0], spread = lax.optimization_barrier((mine, spread))
    for mask in range(0, share, 2):
        pieces[mask + 1] = swap(pieces[mask], 1)
    weights = conv_tiles[0]
    if part % 16:
        for mask in [1 << level for level in range(share.bit_length() - 1)]:
            pieces = [
                jnp.where(index & mask != 0, pieces[j ^ mask], pieces[j]) for j in range(share)
            ]
        steps = [()]
        pieces = [jnp.concatenate(pieces, 1)]
    else:
        steps = [(0, 1, far, far + 1, *near), tuple(mask + 1 for mask in near)]

    before = []
    for i, masks in enumerate(steps):
        first, last = i == 0, i == len(steps) - 1
        parts = [pieces[mask] for mask in masks] or pieces
        depth = sum(block.shape[1] for block in parts)
        outs = [shape((voxels, filters), F32), shape((voxels, filters), BF)]
        if not last:
            outs = [shape((9, voxels, filters), F32)]
        done = local(
            functools.partial(conv_body, share, masks, first, last),
            tuple(outs),
            [pltpu.VMEM((frames_of * depth, voxels), BF)],
            2 * taps * depth * filters * voxels,
            2 * taps * depth * filters,
            me,
            *before,
            weights,
            *parts,
        )
        before = done[:1]
    partial, sent = done
    others = [swap(sent, share * block) for block in range(1, blocks)]
    phases = functools.partial(
        local,
        phase_body,
        shape((min(lines, 2), 2, 4 * filters, outputs), BF),
        [],
        32 * filters * outputs,
        34 * filters * outputs,
        me,
    )
    partial, tiles, mate_tiles = lax.optimization_barrier((partial, up_tiles[0], mate_tiles))
    keep, mate_phases = phases(tiles), phases(mate_tiles)
    others[0], keep, mate_phases = lax.optimization_barrier((others[0], keep, mate_phases))
    hidden = local(
        silu_body,
        shape((voxels, filters), BF),
        [],
        8 * voxels * filters,
        8 * voxels * filters,
        me,
        partial,
        *others,
    )
    mate_hidden = swap(hidden, 1)
    one = (lines, 2 * W, outputs)
    padded = pltpu.VMEM((3, voxels + 2 * W, filters), BF)
    work = 16 * filters * outputs * voxels
    first = local(
        up_first_body,
        shape((halves, *one), F32),
        [padded],
        work,
        16 * filters * outputs,
        me,
        hidden,
        keep,
    )
    own, *leaving = local(
        up_second_body,
        (shape(one, F32),) + (shape(one, BF),) * (halves - 1),
        [pltpu.VMEM((halves, *one), F32), padded],
        work,
        16 * filters * outputs,
        me,
        first,
        mate_hidden,
        mate_phases,
    )
    arrived = [
        swap(block, 2 * mask) for mask, block in zip(farthest_first(halves), leaving, strict=True)
    ]
    return local(
        final_body,
        shape((1, outputs, lines * 2 * W), BF),
        [pltpu.VMEM((lines, max(outputs // 128, 1), 2 * W, 128), F32)],
        own.size,
        12 * own.size,
        me,
        spread,
        own,
        *arrived,
    )


def solution(mesh):
    return jax.shard_map(
        on_device,
        mesh=mesh,
        in_specs=(
            P(("groups", "rows"), None, None),
            P("rows", None, None, None),
            P("rows", None, None, None),
        ),
        out_specs=P(("groups", "rows"), None, None),
        check_vma=False,
    )
```

```python
import functools

import jax
import jax.numpy as jnp
from jax import lax
from jax.experimental import pallas as pl
from jax.experimental.pallas import tpu as pltpu
from jax.sharding import PartitionSpec as P

W = 64
BF = jnp.bfloat16
F32 = jnp.float32
VMEM = pl.BlockSpec(memory_space=pltpu.VMEM)
SMEM = pl.BlockSpec(memory_space=pltpu.SMEM)
LIMIT = 32 * 2**20


def swap(block, mask):
    count = lax.axis_size("rows")
    return lax.ppermute(block, "rows", [(i, i ^ mask) for i in range(count)])


def local(body, outs, scratch, flops, moved, me, *args):
    return pl.pallas_call(
        body,
        out_shape=outs,
        in_specs=[SMEM] + [VMEM] * len(args),
        out_specs=jax.tree.map(lambda _: VMEM, outs),
        scratch_shapes=scratch,
        compiler_params=pltpu.CompilerParams(vmem_limit_bytes=LIMIT),
        cost_estimate=pl.CostEstimate(flops=flops, bytes_accessed=moved, transcendentals=0),
    )(me, *args)


def farthest_first(chips):
    return (chips - 1, *range(1, chips - 1))


def phase_groups(phase):
    if phase == 0:
        return [(-1, (0,)), (0, (1, 2))]
    return [(0, (0, 1)), (1, (2,))]


def shift_cols(plane, step):
    if step == 0:
        return plane
    voxels = plane.shape[0]
    col = lax.broadcasted_iota(jnp.int32, plane.shape, 0) % W
    rolled = pltpu.roll(plane, (-step) % voxels, 0)
    return jnp.where((col + step >= 0) & (col + step < W), rolled, 0)


def shift_rows(plane, step):
    if step == 0:
        return plane
    zeros = jnp.zeros((W,) + plane.shape[1:], plane.dtype)
    if step > 0:
        return jnp.concatenate([plane[W:], zeros], 0)
    return jnp.concatenate([zeros, plane[:-W]], 0)


def phase_body(me_ref, tiles_ref, out_ref):
    upper = me_ref[0] % 2 == 1
    taps = [tiles_ref[t].astype(F32).T for t in range(9)]
    depth = taps[0].shape[0]
    for q in range(2):
        place = 0
        for u in range(2):
            for _, col_taps in phase_groups(q):
                rows = slice(place * depth, (place + 1) * depth)
                place += 1
                totals = []
                for p in range(2):
                    total = None
                    for b in phase_groups(p)[u][1]:
                        for e in col_taps:
                            tap = taps[3 * b + e]
                            total = tap if total is None else total + tap
                    totals.append(total)
                if out_ref.shape[0] == 1:
                    totals = [jnp.where(upper, totals[1], totals[0])]
                for p, total in enumerate(totals):
                    out_ref[p, q, rows, :] = total.astype(BF)


def conv_body(share, masks, first, last, me_ref, *refs):
    refs = list(refs)
    before_ref = None if first else refs.pop(0)
    weight_ref = refs.pop(0)
    pieces = [refs.pop(0) for _ in masks or (0,)]
    *out_refs, order_ref = refs
    frames_of, _, voxels = pieces[0].shape
    channels = order_ref.shape[0] // frames_of
    if masks:
        part = weight_ref.shape[1] // share
        me = me_ref[0] % share
        spans = [pl.ds(pl.multiple_of((me ^ mask) * part, part), part) for mask in masks]
    else:
        spans = [slice(None)]
    for a in range(frames_of):
        for i, piece_ref in enumerate(pieces):
            place = a * channels + i * piece_ref.shape[1]
            order_ref[place : place + piece_ref.shape[1], :] = piece_ref[a]
    columns = order_ref[...].T
    products = [None] * 9
    for low in range(0, 9, 2):
        pair = range(low, min(low + 2, 9))
        weights = jnp.concatenate(
            [
                jnp.concatenate(
                    [weight_ref[9 * a + t, span, :] for a in range(frames_of) for span in spans], 0
                )
                for t in pair
            ],
            1,
        )
        product = jnp.dot(columns, weights, preferred_element_type=F32)
        filters = product.shape[1] // len(pair)
        for i, t in enumerate(pair):
            own = product[:, i * filters : (i + 1) * filters]
            products[t] = own if first else before_ref[t] + own
    if not last:
        for t in range(9):
            out_refs[0][t] = products[t]
        return
    total = None
    for e in range(3):
        rows = sum(shift_rows(products[3 * b + e], b - 1) for b in range(3))
        moved = shift_cols(rows, e - 1)
        total = moved if total is None else total + moved
    out_refs[0][...] = total
    out_refs[1][...] = total.astype(BF)


def silu_body(me_ref, *refs):
    *sum_refs, hidden_ref = refs
    pre = sum_refs[0][...]
    for other_ref in sum_refs[1:]:
        pre = pre + other_ref[...].astype(F32)
    hidden_ref[...] = (pre / (1 + jnp.exp(-pre))).astype(BF)


def up_products(me_ref, hidden_ref, weight_ref, padded_ref, halves, lines):
    hidden = hidden_ref[...].astype(F32)
    voxels = hidden.shape[0]
    for i, v in enumerate((-1, 0, 1)):
        edge = jnp.zeros((W, hidden.shape[1]), BF)
        padded_ref[i, :W, :] = edge
        padded_ref[i, W + voxels :, :] = edge
        plane = shift_cols(hidden, v).astype(BF) if v else hidden_ref[...]
        padded_ref[i, W : W + voxels, :] = plane
    upper = me_ref[0] % 2
    if lines == 1:
        blocks = [(0, halves, upper, [(half, 0) for half in range(halves)])]
    else:
        blocks = [
            (
                p,
                lines // 2,
                half * lines + upper * (lines // 2) + p,
                [(half, 2 * i + p) for i in range(lines // 2)],
            )
            for half in range(halves)
            for p in range(2)
        ]
    for p, count, base, places in blocks:
        for q in range(2):
            columns = []
            for u in range(2):
                start = pl.multiple_of((base + u) * W, W)
                for v, _ in phase_groups(q):
                    columns.append(padded_ref[v + 1, pl.ds(start, count * W), :])
            product = jnp.dot(
                jnp.concatenate(columns, 1), weight_ref[p, q], preferred_element_type=F32
            )
            for i, (half, k) in enumerate(places):
                yield half, k, slice(q * W, (q + 1) * W), product[i * W : (i + 1) * W]


def up_first_body(me_ref, hidden_ref, weight_ref, out_ref, padded_ref):
    halves, lines = out_ref.shape[:2]
    for half, k, cells, value in up_products(
        me_ref, hidden_ref, weight_ref, padded_ref, halves, lines
    ):
        out_ref[half, k, cells, :] = value


def up_second_body(me_ref, before_ref, hidden_ref, weight_ref, *refs):
    *out_refs, total_ref, padded_ref = refs
    halves, lines = before_ref.shape[:2]
    for half, k, cells, value in up_products(
        me_ref, hidden_ref, weight_ref, padded_ref, halves, lines
    ):
        total_ref[half, k, cells, :] = before_ref[half, k, cells, :] + value
    chip = me_ref[0] // 2 % halves
    own_ref, *leaving_refs = out_refs
    own_ref[...] = total_ref[chip]
    for mask, out_ref in zip(farthest_first(halves), leaving_refs, strict=True):
        out_ref[...] = total_ref[chip ^ mask].astype(BF)


def spread_body(me_ref, out_ref):
    cell = lax.broadcasted_iota(jnp.int32, out_ref.shape, 0)
    place = lax.broadcasted_iota(jnp.int32, out_ref.shape, 1)
    out_ref[...] = (place == 2 * (cell % W) + cell // W).astype(BF)


def final_body(me_ref, spread_ref, own_ref, *refs):
    *other_refs, out_ref, line_ref = refs
    total = own_ref[...]
    for other_ref in other_refs:
        total = total + other_ref[...].astype(F32)
    total = total.astype(BF)
    outputs = total.shape[2]
    for k in range(total.shape[0]):
        places = slice(k * 2 * W, (k + 1) * 2 * W)
        whole = outputs // 128
        for i in range(whole):
            block = total[k, :, i * 128 : (i + 1) * 128].astype(F32)
            for q in range(2):
                line_ref[k, i, pl.ds(q, W, stride=2), :] = block[q * W : (q + 1) * W]
        for i in range(whole):
            out_ref[0, i * 128 : (i + 1) * 128, places] = line_ref[k, i].T.astype(BF)
        if outputs % 128:
            woven = lax.dot_general(
                total[k, :, whole * 128 :],
                spread_ref[...],
                (((0,), (0,)), ((), ())),
                preferred_element_type=F32,
            )
            out_ref[0, whole * 128 :, places] = woven.astype(BF)


def on_device(frames, conv_tiles, up_tiles):
    index = lax.axis_index("rows")
    me = index.reshape(1).astype(jnp.int32)
    count = lax.axis_size("rows")
    part, frames_of, voxels = frames.shape
    taps, channels, filters = conv_tiles.shape[1:]
    outputs = up_tiles.shape[2]
    share = channels // part
    blocks = count // share
    halves = share // 2
    lines = 2 * (voxels // W) // share
    shape = jax.ShapeDtypeStruct

    mine = frames.transpose(1, 0, 2)
    pieces = [mine] + [None] * (share - 1)
    far = share - 2
    near = list(range(2, far, 2))
    for mask in range(2, share, 2):
        pieces[mask] = swap(mine, mask)
    spread = local(spread_body, shape((2 * W, 2 * W), BF), [], 2**33, 2**25, me)
    mate_tiles = swap(up_tiles[0], 1)
    pieces[far], spread, mate_tiles = lax.optimization_barrier(
        (pieces[far], spread, mate_tiles)
    )
    pieces[0], spread = lax.optimization_barrier((mine, spread))
    for mask in range(0, share, 2):
        pieces[mask + 1] = swap(pieces[mask], 1)
    weights = conv_tiles[0]
    if part % 16:
        for mask in [1 << level for level in range(share.bit_length() - 1)]:
            pieces = [
                jnp.where(index & mask != 0, pieces[j ^ mask], pieces[j]) for j in range(share)
            ]
        steps = [()]
        pieces = [jnp.concatenate(pieces, 1)]
    else:
        steps = [(0, far, *near, 1, far + 1), tuple(mask + 1 for mask in near)]

    before = []
    for i, masks in enumerate(steps):
        first, last = i == 0, i == len(steps) - 1
        parts = [pieces[mask] for mask in masks] or pieces
        depth = sum(block.shape[1] for block in parts)
        outs = [shape((voxels, filters), F32), shape((voxels, filters), BF)]
        if not last:
            outs = [shape((9, voxels, filters), F32)]
        done = local(
            functools.partial(conv_body, share, masks, first, last),
            tuple(outs),
            [pltpu.VMEM((frames_of * depth, voxels), BF)],
            2 * taps * depth * filters * voxels,
            2 * taps * depth * filters,
            me,
            *before,
            weights,
            *parts,
        )
        before = done[:1]
    partial, sent = done
    others = [swap(sent, share * block) for block in range(1, blocks)]
    phases = functools.partial(
        local,
        phase_body,
        shape((min(lines, 2), 2, 4 * filters, outputs), BF),
        [],
        32 * filters * outputs,
        34 * filters * outputs,
        me,
    )
    partial, tiles, mate_tiles = lax.optimization_barrier((partial, up_tiles[0], mate_tiles))
    keep, mate_phases = phases(tiles), phases(mate_tiles)
    others[0], keep, mate_phases = lax.optimization_barrier((others[0], keep, mate_phases))
    hidden = local(
        silu_body,
        shape((voxels, filters), BF),
        [],
        8 * voxels * filters,
        8 * voxels * filters,
        me,
        partial,
        *others,
    )
    mate_hidden = swap(hidden, 1)
    one = (lines, 2 * W, outputs)
    padded = pltpu.VMEM((3, voxels + 2 * W, filters), BF)
    work = 16 * filters * outputs * voxels
    first = local(
        up_first_body,
        shape((halves, *one), F32),
        [padded],
        work,
        16 * filters * outputs,
        me,
        hidden,
        keep,
    )
    own, *leaving = local(
        up_second_body,
        (shape(one, F32),) + (shape(one, BF),) * (halves - 1),
        [pltpu.VMEM((halves, *one), F32), padded],
        work,
        16 * filters * outputs,
        me,
        first,
        mate_hidden,
        mate_phases,
    )
    arrived = [
        swap(block, 2 * mask) for mask, block in zip(farthest_first(halves), leaving, strict=True)
    ]
    return local(
        final_body,
        shape((1, outputs, lines * 2 * W), BF),
        [pltpu.VMEM((lines, max(outputs // 128, 1), 2 * W, 128), F32)],
        own.size,
        12 * own.size,
        me,
        spread,
        own,
        *arrived,
    )


def solution(mesh):
    return jax.shard_map(
        on_device,
        mesh=mesh,
        in_specs=(
            P(("groups", "rows"), None, None),
            P("rows", None, None, None),
            P("rows", None, None, None),
        ),
        out_specs=P(("groups", "rows"), None, None),
        check_vma=False,
    )
```
